512 devices in a mesh: ctx: 32 (over y_hi, z, core), dp: 16 (over x, y_lo).
Axes of the slice: x: 4, y: 8 (y_hi: 2, y_lo: 4; y = y_hi * 4 + y_lo), z: 8, core: 2. Of those that a mesh axis runs over, the one named last changes fastest.
Arguments:
- queries: bfloat16 [16, 2048, 2560], P('dp', 'ctx'), may hold values from -144 to 144
- output_gradient: bfloat16 [16, 2048, 2560], P('dp', 'ctx'), may hold values from -6 to 6
- attention_output: bfloat16 [16, 2048, 2560], P('dp', 'ctx'), may hold values from -3 to 3
- completion_key_rows: bfloat16 [16, 2048, 512], P('dp', 'ctx'), may hold values from -6 to 6
- completion_value_rows: bfloat16 [16, 2048, 512], P('dp', 'ctx'), may hold values from -6 to 6
- prompt_keys: bfloat16 [16, 2048, 512], P('dp', 'ctx'), may hold values from -6 to 6
- prompt_value_rows: bfloat16 [16, 2048, 512], P('dp', 'ctx'), may hold values from -6 to 6
- prompt_states: bfloat16 [16, 2048, 5120], P('dp', None, 'ctx'), may hold values from -6 to 6
- comp_lengths: int32 [16, 32, 4], P('dp', 'ctx'), may hold values from 1 to 32, 64 in all within a row
Outputs:
- grad_query: bfloat16 [16, 2048, 2560], P('dp', 'ctx')
- grad_comp_keys: bfloat16 [16, 2048, 512], P('dp', 'ctx')
- grad_comp_values: bfloat16 [16, 2048, 512], P('dp', 'ctx')
- grad_prompt_keys: bfloat16 [16, 2048, 512], P('dp', 'ctx')
- grad_prompt_values: bfloat16 [16, 2048, 512], P('dp', 'ctx')
- grad_proj: float32 [5120, 512], P('ctx', 'dp')
The draws below stay inside these ranges and needn't reach their ends.
Inputs may be any that keep to these rules, and one draw needn't show every extreme that they name: `comp_lengths`: the 4 lengths of one device sum to 64.
All inputs are finite; a program needn't handle non-finite values.
Results may differ from the reference program's by a relative error of at most 0.0051.
Values may be sent and summed in bfloat16 or wider, within the bound.
A program may use at most 128 MiB of HBM per device.

```python
import math
import jax
import jax.numpy as jnp
import numpy as np
from jax import lax

D = 5120
QUERY_HEAD_COUNT = 20
KEY_HEAD_COUNT = 4
HEAD_SIZE = 128
SLOTS = 4
DEVICE_TOKENS = 64
PROMPT_LENGTH = 2048
COMPLETION_LENGTH = 2048
PROMPT_GROUPS = 16
N_CTX = 32


def drawn_pair(key):
    random_key_sample = jnp.clip(jax.random.normal(jax.random.fold_in(key, 11), (PROMPT_GROUPS, PROMPT_LENGTH, KEY_HEAD_COUNT * HEAD_SIZE), jnp.float32), -6.0, 6.0)
    query_draw = jnp.clip(jax.random.normal(jax.random.fold_in(key, 12), (PROMPT_GROUPS, COMPLETION_LENGTH, QUERY_HEAD_COUNT * HEAD_SIZE), jnp.float32), -6.0, 6.0)
    return (random_key_sample, query_draw)


def draw_prompt_keys(key, part):
    return drawn_pair(key)[0].astype(jnp.bfloat16)


def draw_queries(key, part):
    return drawn_pair(key)[1].astype(jnp.bfloat16)


def levels(rng, shape, cuts, smallest, top_value):
    gain = 1.0
    for axis_at, blocks in cuts:
        steps = jax.random.uniform(jax.random.fold_in(jax.random.fold_in(rng, 6), axis_at), (blocks,), jnp.float32, smallest / len(cuts), top_value / len(cuts))
        gain = gain * jnp.repeat(jnp.exp(steps), shape[axis_at] // blocks).reshape((-1,) + (1,) * (len(shape) - 1 - axis_at))
    return gain


def profile(count, total, reach, slope):
    loads = [(1 << 20) // math.isqrt(standing ** slope) + 1 for standing in range(2, count + 1)]
    spare, holding = total - reach - (count - 1), [1] * (count - 1)
    while spare > 0:
        candidates = [i for i in range(count - 1) if holding[i] < reach]
        whole, remaining = sum([loads[i] for i in candidates]), spare
        for i in candidates:
            extra = min(reach - holding[i], max(1, remaining * loads[i] // whole), spare)
            holding[i] = holding[i] + extra
            spare = spare - extra
    return np.array([reach] + holding)


def uneven_parts(own_key, count, total, limit, slope):
    if count == 2:
        one = jax.random.randint(own_key, (), max(1, total - limit), min(limit, total - 1) + 1)
        return jnp.stack([one, total - one])
    sizes = jnp.asarray(profile(count, total, limit, slope), jnp.int32)
    twos = (count - 1) // 2
    giver, sink = sizes[1:1 + 2 * twos:2], sizes[2:2 + 2 * twos:2]
    margin = jnp.minimum(giver - 1, limit - sink)
    shifted = jax.random.randint(jax.random.fold_in(own_key, 1), (twos,), 0, 1 << 20) % (margin + 1)
    sizes = sizes.at[1:1 + 2 * twos:2].set(giver - shifted).at[2:2 + 2 * twos:2].set(sink + shifted)
    return sizes[jax.random.permutation(jax.random.fold_in(own_key, 2), count)]


def scatter_about(key, dims, scale, most, split=(), kind=jnp.bfloat16):
    result = jax.random.normal(key, dims, jnp.float32) * scale
    if len(split) > 0:
        result = levels(key, dims, split, -0.22, 0.18) * result
    return jnp.clip(result, min=-most, max=most).astype(kind)


def setup_inputs(seed: int = 0) -> dict:
    keys = jax.random.split(jax.random.key(seed), 10)
    queries = draw_queries(jax.random.fold_in(keys[9], 71), 0)
    output_gradient = scatter_about(keys[1], (PROMPT_GROUPS, COMPLETION_LENGTH, QUERY_HEAD_COUNT * HEAD_SIZE), 1.0, 6.0, ((0, 16), (1, 32)))
    attention_output = scatter_about(keys[2], (PROMPT_GROUPS, COMPLETION_LENGTH, QUERY_HEAD_COUNT * HEAD_SIZE), 0.5, 3.0, ((0, 16), (1, 32)))
    completion_key_rows = scatter_about(keys[3], (PROMPT_GROUPS, COMPLETION_LENGTH, KEY_HEAD_COUNT * HEAD_SIZE), 1.0, 6.0, ((0, 16), (1, 32)))
    completion_value_rows = scatter_about(keys[4], (PROMPT_GROUPS, COMPLETION_LENGTH, KEY_HEAD_COUNT * HEAD_SIZE), 1.0, 6.0, ((0, 16), (1, 32)))
    prompt_keys = draw_prompt_keys(jax.random.fold_in(keys[9], 71), 0)
    prompt_value_rows = scatter_about(keys[6], (PROMPT_GROUPS, PROMPT_LENGTH, KEY_HEAD_COUNT * HEAD_SIZE), 1.0, 6.0, ((0, 16), (1, 32)))
    prompt_states = scatter_about(keys[7], (PROMPT_GROUPS, PROMPT_LENGTH, D), 1.0, 6.0, ((0, 16), (2, 32)))
    comp_lengths = jax.vmap(lambda own: uneven_parts(own, SLOTS, DEVICE_TOKENS, DEVICE_TOKENS // 2, 2))(jax.random.split(keys[8], PROMPT_GROUPS * N_CTX)).reshape((PROMPT_GROUPS, N_CTX, SLOTS)).astype(jnp.int32)
    return dict(queries=queries, output_gradient=output_gradient, attention_output=attention_output, completion_key_rows=completion_key_rows, completion_value_rows=completion_value_rows, prompt_keys=prompt_keys, prompt_value_rows=prompt_value_rows, prompt_states=prompt_states, comp_lengths=comp_lengths)


MASKED = -1.0e30


def visible_mask(token_lengths, local_rows):
    slot_ends = jnp.cumsum(token_lengths).astype(jnp.int32)
    position = jnp.arange(local_rows, dtype=jnp.int32)
    segment = jnp.sum((position[:, None] >= slot_ends[None, :]).astype(jnp.int32), axis=1)
    return (segment[:, None] == segment[None, :]) & (position[None, :] <= position[:, None])


def device_block(query_row_block, cotangent_row_block, saved_row_block, completion_key, completion_value, prompt_key_block, prompt_value_block, token_lengths):
    group_length = QUERY_HEAD_COUNT // KEY_HEAD_COUNT
    local_rows = query_row_block.shape[0]
    scale = HEAD_SIZE ** -0.5
    heads_of_query = query_row_block.astype(jnp.float32).reshape(local_rows, KEY_HEAD_COUNT, group_length, HEAD_SIZE)
    cotangent_by_head = cotangent_row_block.astype(jnp.float32).reshape(local_rows, KEY_HEAD_COUNT, group_length, HEAD_SIZE)
    saved_by_head = saved_row_block.astype(jnp.float32).reshape(local_rows, KEY_HEAD_COUNT, group_length, HEAD_SIZE)
    heads_of_key = jnp.concatenate([prompt_key_block, completion_key], axis=0).astype(jnp.float32).reshape(-1, KEY_HEAD_COUNT, HEAD_SIZE)
    heads_of_value = jnp.concatenate([prompt_value_block, completion_value], axis=0).astype(jnp.float32).reshape(-1, KEY_HEAD_COUNT, HEAD_SIZE)
    seen = jnp.concatenate([jnp.ones((local_rows, prompt_key_block.shape[0]), dtype=jnp.bool_), visible_mask(token_lengths, local_rows)], axis=1)
    scores = jnp.einsum("chgd,khd->chgk", heads_of_query, heads_of_key) * scale
    scores = jnp.where(seen[:, None, None, :], scores, MASKED)
    row_top = jnp.max(scores, axis=-1)
    log_total = row_top + jnp.log(jnp.sum(jnp.exp(scores - row_top[..., None]), axis=-1))
    softmax_p = jnp.exp(scores - log_total[..., None])
    row_delta = jnp.sum(cotangent_by_head * saved_by_head, axis=-1)
    dprobs = jnp.einsum("chgd,khd->chgk", cotangent_by_head, heads_of_value)
    dscores = softmax_p * (dprobs - row_delta[..., None])
    probs_bf = lax.optimization_barrier(softmax_p.astype(jnp.bfloat16)).astype(jnp.float32)
    dscores_bf = lax.optimization_barrier(dscores.astype(jnp.bfloat16)).astype(jnp.float32)
    query_gradient = jnp.einsum("chgk,khd->chgd", dscores_bf, heads_of_key) * scale
    key_gradient = jnp.einsum("chgk,chgd->khd", dscores_bf, heads_of_query) * scale
    value_gradient = jnp.einsum("chgk,chgd->khd", probs_bf, cotangent_by_head)
    return query_gradient.reshape(local_rows, QUERY_HEAD_COUNT * HEAD_SIZE), key_gradient.reshape(-1, KEY_HEAD_COUNT * HEAD_SIZE), value_gradient.reshape(-1, KEY_HEAD_COUNT * HEAD_SIZE)


def reference(queries, output_gradient, attention_output, completion_key_rows, completion_value_rows, prompt_keys, prompt_value_rows, prompt_states, comp_lengths):
    def one_group(group_items):
        query_all, cotangent_all, saved_output_all, completion_key, completion_value, prompt_key_block, prompt_value_block, states, token_lengths = group_items
        block_items = (query_all.reshape(N_CTX, DEVICE_TOKENS, QUERY_HEAD_COUNT * HEAD_SIZE), cotangent_all.reshape(N_CTX, DEVICE_TOKENS, QUERY_HEAD_COUNT * HEAD_SIZE),
                       saved_output_all.reshape(N_CTX, DEVICE_TOKENS, QUERY_HEAD_COUNT * HEAD_SIZE), completion_key.reshape(N_CTX, DEVICE_TOKENS, KEY_HEAD_COUNT * HEAD_SIZE),
                       completion_value.reshape(N_CTX, DEVICE_TOKENS, KEY_HEAD_COUNT * HEAD_SIZE), token_lengths)

        def one_block(items):
            return device_block(items[0], items[1], items[2], items[3], items[4], prompt_key_block, prompt_value_block, items[5])

        query_gradient, key_gradient, value_gradient = lax.map(one_block, block_items)
        prompt_gk = jnp.sum(key_gradient[:, :PROMPT_LENGTH], axis=0).astype(jnp.bfloat16)
        prompt_gv = jnp.sum(value_gradient[:, :PROMPT_LENGTH], axis=0).astype(jnp.bfloat16)
        completion_key_gradient = key_gradient[:, PROMPT_LENGTH:].reshape(COMPLETION_LENGTH, KEY_HEAD_COUNT * HEAD_SIZE).astype(jnp.bfloat16)
        completion_value_gradient = value_gradient[:, PROMPT_LENGTH:].reshape(COMPLETION_LENGTH, KEY_HEAD_COUNT * HEAD_SIZE).astype(jnp.bfloat16)
        projection = jnp.dot(states.T, prompt_gk, preferred_element_type=jnp.float32)
        return query_gradient.reshape(COMPLETION_LENGTH, QUERY_HEAD_COUNT * HEAD_SIZE).astype(jnp.bfloat16), completion_key_gradient, completion_value_gradient, prompt_gk, prompt_gv, projection

    results = lax.map(one_group, (queries, output_gradient, attention_output, completion_key_rows, completion_value_rows, prompt_keys, prompt_value_rows, prompt_states, comp_lengths))
    return results[0], results[1], results[2], results[3], results[4], jnp.sum(results[5], axis=0)
```

```python
import functools
import math

import jax
import jax.numpy as jnp
from jax import lax
from jax.experimental import pallas as pl
from jax.experimental.pallas import tpu as pltpu
from jax.sharding import PartitionSpec as P

QUERY_HEAD_COUNT = 20
KEY_HEAD_COUNT = 4
HEAD_SIZE = 128
GROUP = QUERY_HEAD_COUNT // KEY_HEAD_COUNT
MASKED = -1e30
SCALE = HEAD_SIZE ** (-0.5)
LOG2E = math.log2(math.e)
MESH = pl.DeviceIdType.MESH
F32 = jnp.float32
BF16 = jnp.bfloat16

HEADS = KEY_HEAD_COUNT // 2
KW = HEADS * HEAD_SIZE
QW = HEADS * GROUP * HEAD_SIZE
T = 64
ROWS = GROUP * 2 * T
BLOCK = 2 * T


def dot(a, b, ca=1, cb=0):
    return lax.dot_general(a, b, (((ca,), (cb,)), ((), ())), preferred_element_type=F32)


def kernel(
    n_z,
    n_dp,
    q_in,
    do_in,
    o_in,
    kc_in,
    vc_in,
    pk_in,
    pv_in,
    st_in,
    len_in,
    gq_out,
    gkc_out,
    gvc_out,
    gpk_out,
    gpv_out,
    gproj_out,
    kvb,
    raw,
    kvc,
    bias_own,
    bias,
    st,
    qs,
    dos,
    q_t,
    do_t,
    delta,
    top,
    total,
    sbuf,
    sc,
    dq_t,
    part,
    sb,
    rb,
    yb,
    dkb,
    dvf,
    proj,
    prx,
    gqs,
    gkvc,
    loc,
    sib_s,
    sib_r,
    y_s,
    y_r,
    kv_s,
    kv_r,
    rs_s,
    rs_r,
    dk_s,
    dk_r,
    pj_s,
    pj_r,
    ret_s,
    ret_r,
):
    half = n_z // 2
    per_core = n_dp // 2
    cols = KEY_HEAD_COUNT * HEAD_SIZE // n_dp
    c = lax.axis_index("ctx")
    g = lax.axis_index("dp")
    core = lax.rem(c, 2)
    z = lax.rem(c // 2, n_z)
    y = c // (2 * n_z)
    base = y * (2 * n_z)
    sib = c + 1 - 2 * core
    ypart = (1 - y) * (2 * n_z) + z * 2 + core
    right = base + lax.rem(z + 1, n_z) * 2 + core
    left = base + lax.rem(z + n_z - 1, n_z) * 2 + core
    ring = (right, left)

    def remote(src, dst, s_sem, r_sem, ctx, dp=None):
        return pltpu.make_async_remote_copy(
            src_ref=src,
            dst_ref=dst,
            send_sem=s_sem,
            recv_sem=r_sem,
            device_id=(ctx, g if dp is None else dp),
            device_id_type=MESH,
        )

    def greet(ctx, dp):
        pl.semaphore_signal(
            pltpu.get_barrier_semaphore(), inc=1, device_id=(ctx, dp), device_id_type=MESH
        )

    for other in (sib, ypart, right, left):
        greet(other, g)
    src_core = g // per_core
    src_ctx = c - core + src_core

    def greet_source(i, carry):
        @pl.when(jnp.logical_or(src_ctx != c, i != g))
        def _():
            greet(src_ctx, i)

        return carry

    lax.fori_loop(0, n_dp, greet_source, 0)

    own_q = pl.ds(pl.multiple_of(core * QW, 128), QW)
    sib_q = pl.ds(pl.multiple_of((1 - core) * QW, 128), QW)
    own_k = pl.ds(pl.multiple_of(core * KW, 128), KW)
    sib_k = pl.ds(pl.multiple_of((1 - core) * KW, 128), KW)
    own_rows = pl.ds(pl.multiple_of(core * T, T), T)
    sib_rows = pl.ds(pl.multiple_of((1 - core) * T, T), T)
    copies = [
        pltpu.make_async_copy(pk_in.at[:, own_k], kvb.at[z, 0, 0, own_rows], loc.at[0]),
        pltpu.make_async_copy(pv_in.at[:, own_k], kvb.at[z, 0, 1, own_rows], loc.at[1]),
        pltpu.make_async_copy(q_in.at[:, own_q], raw.at[0, 0], loc.at[2]),
        pltpu.make_async_copy(do_in.at[:, own_q], raw.at[1, 0], loc.at[3]),
        pltpu.make_async_copy(o_in.at[:, own_q], raw.at[2, 0], loc.at[4]),
        pltpu.make_async_copy(kc_in.at[:, own_k], kvc.at[0, pl.ds(0, T)], loc.at[5]),
        pltpu.make_async_copy(vc_in.at[:, own_k], kvc.at[1, pl.ds(0, T)], loc.at[6]),
        pltpu.make_async_copy(st_in, st.at[0], loc.at[7]),
    ]
    for copy in copies:
        copy.start()

    key_at = lax.broadcasted_iota(jnp.int32, (T, 2 * T), 0)
    lane = lax.broadcasted_iota(jnp.int32, (T, 2 * T), 1)
    end0 = len_in[0]
    end1 = end0 + len_in[1]
    end2 = end1 + len_in[2]

    def slot(position):
        return (
            (position >= end0).astype(jnp.int32)
            + (position >= end1).astype(jnp.int32)
            + (position >= end2).astype(jnp.int32)
        )

    def shifted(offset):
        token = lane - offset
        seen = (token >= 0) & (token < T) & (key_at <= token) & (slot(key_at) == slot(token))
        return jnp.where(seen, 0.0, MASKED).astype(BF16)

    bias[0:T, :] = shifted(0)
    bias_own[...] = shifted(T)

    self_target = (src_core == core).astype(jnp.int32)
    pl.semaphore_wait(pltpu.get_barrier_semaphore(), 4 + n_dp - self_target)

    pairs = [
        (pk_in.at[:, sib_k], kvb.at[z, 0, 0, own_rows], kvb.at[z, 0, 0, sib_rows]),
        (pv_in.at[:, sib_k], kvb.at[z, 0, 1, own_rows], kvb.at[z, 0, 1, sib_rows]),
        (q_in.at[:, sib_q], raw.at[0, 1], raw.at[0, 1]),
        (do_in.at[:, sib_q], raw.at[1, 1], raw.at[1, 1]),
        (o_in.at[:, sib_q], raw.at[2, 1], raw.at[2, 1]),
        (kc_in.at[:, sib_k], kvc.at[0, pl.ds(T, T)], kvc.at[0, pl.ds(T, T)]),
        (vc_in.at[:, sib_k], kvc.at[1, pl.ds(T, T)], kvc.at[1, pl.ds(T, T)]),
        (bias_own, bias.at[pl.ds(T, T)], bias.at[pl.ds(T, T)]),
        (st_in, st.at[1], st.at[1]),
    ]
    sends = [
        remote(src, dst, sib_s.at[i], sib_r.at[i], sib) for i, (src, dst, _) in enumerate(pairs)
    ]
    lands = [
        remote(land, land, sib_s.at[i], sib_r.at[i], sib) for i, (_, _, land) in enumerate(pairs)
    ]
    for send in sends:
        send.start()

    def hops(d, r):
        return half - r if d == 0 else half - 1 + r

    def place(d, s):
        return lax.rem(z + (n_z - s if d == 0 else s), n_z)

    def gather_send(buf, s_sem, r_sem, d, r, s):
        block = buf.at[place(d, s), r]
        return remote(block, block, s_sem.at[d, r, s + 1], r_sem.at[d, r, s + 1], ring[d])

    def gather_land(buf, s_sem, r_sem, d, r, s):
        block = buf.at[place(d, s), r]
        return remote(block, block, s_sem.at[d, r, s], r_sem.at[d, r, s], ring[d])

    def gather_start(buf, s_sem, r_sem, slot_y):
        across = remote(buf.at[z, 0], buf.at[z, 1], y_s.at[slot_y], y_r.at[slot_y], ypart)
        across.start()
        for d in (0, 1):
            gather_send(buf, s_sem, r_sem, d, 0, 0).start()
        return across

    def gather_across(buf, s_sem, r_sem, across):
        across.wait_recv()
        for d in (0, 1):
            gather_send(buf, s_sem, r_sem, d, 1, 0).start()

    def gather_step(buf, s_sem, r_sem, s):
        for r in (0, 1):
            for d in (0, 1):

                @pl.when(s <= hops(d, r))
                def _():
                    gather_land(buf, s_sem, r_sem, d, r, s).wait_recv()

                @pl.when(s < hops(d, r))
                def _():
                    gather_send(buf, s_sem, r_sem, d, r, s).start()

    def gather_drain(buf, s_sem, r_sem, across):
        across.wait_send()
        for d in (0, 1):
            for r in (0, 1):

                def drain(s, carry):
                    gather_send(buf, s_sem, r_sem, d, r, s).wait_send()
                    return carry

                lax.fori_loop(0, hops(d, r), drain, 0)

    def spots(s):
        return jnp.where((s == 0) | (s == half), 1, 2)

    for i in (0, 1):
        copies[i].wait()
        lands[i].wait_recv()
    kv_across = gather_start(kvb, kv_s, kv_r, 0)

    for i in (2, 3, 4):
        copies[i].wait()
        lands[i].wait_recv()
    for h in range(HEADS):
        for j in range(GROUP):
            at = (h * GROUP + j) * HEAD_SIZE
            rows = slice(j * BLOCK, (j + 1) * BLOCK)
            q_tile = jnp.concatenate([raw[0, 0, :, at : at + 128], raw[0, 1, :, at : at + 128]], 0)
            do_tile = jnp.concatenate([raw[1, 0, :, at : at + 128], raw[1, 1, :, at : at + 128]], 0)
            o_tile = jnp.concatenate([raw[2, 0, :, at : at + 128], raw[2, 1, :, at : at + 128]], 0)
            qs[h, rows, :] = q_tile
            dos[h, rows, :] = do_tile
            q_t[h, :, rows] = q_tile.T
            do_t[h, :, rows] = do_tile.T
            product = do_tile.astype(F32) * o_tile.astype(F32)
            delta[h, :, rows] = jnp.sum(product.T, axis=0, keepdims=True)

    def merge(h, scores):
        old = top[h]
        new = jnp.maximum(old, jnp.max(scores, axis=0, keepdims=True))
        total[h] = total[h] * jnp.exp2(old - new) + jnp.sum(
            jnp.exp2(scores - new), axis=0, keepdims=True
        )
        top[h] = new

    for i in (5, 6):
        copies[i].wait()
        lands[i].wait_recv()
    lands[7].wait_recv()
    mask_tile = bias[...].astype(F32)
    for h in range(HEADS):
        scores = dot(kvc[0, :, h * 128 : (h + 1) * 128], q_t[h]) * (SCALE * LOG2E)
        scores = scores + jnp.concatenate([mask_tile] * GROUP, axis=1)
        sc[h] = scores
        new = jnp.max(scores, axis=0, keepdims=True)
        top[h] = new
        total[h] = jnp.sum(jnp.exp2(scores - new), axis=0, keepdims=True)
        dq_t[h] = jnp.zeros((HEAD_SIZE, ROWS), F32)

    def first_pass(s):
        def one(i, carry):
            pos = lax.rem(z + n_z + (1 - 2 * i) * s, n_z)
            for h in range(HEADS):
                keys = kvb[pos, :, 0, :, h * 128 : (h + 1) * 128].reshape(2 * BLOCK, HEAD_SIZE)
                scores = dot(keys, q_t[h]) * (SCALE * LOG2E)
                sbuf[h, pos] = scores
                merge(h, scores)
            return carry

        lax.fori_loop(0, spots(s), one, 0)

    gather_across(kvb, kv_s, kv_r, kv_across)

    def kv_slot(s, carry):
        @pl.when(s > 0)
        def _():
            gather_step(kvb, kv_s, kv_r, s)

        first_pass(s)
        return carry

    lax.fori_loop(0, half + 1, kv_slot, 0)
    for h in range(HEADS):
        top[h] = top[h] + jnp.log2(total[h])

    def key_terms(h, scores, keys, values):
        probs = jnp.exp2(scores - top[h])
        dprobs = dot(values, do_t[h])
        dscores = (probs * (dprobs - delta[h])).astype(BF16)
        dv = dot(probs.astype(BF16), dos[h])
        dk = dot(dscores, qs[h]) * SCALE
        dq_t[h] += dot(keys, dscores, 0, 0)
        return dk, dv

    def second_pass(s):
        def one(i, carry):
            pos = lax.rem(z + n_z + (1 - 2 * i) * s, n_z)
            for h in range(HEADS):
                lanes = slice(h * 128, (h + 1) * 128)
                keys = kvb[pos, :, 0, :, lanes].reshape(2 * BLOCK, HEAD_SIZE)
                values = kvb[pos, :, 1, :, lanes].reshape(2 * BLOCK, HEAD_SIZE)
                dk, dv = key_terms(h, sbuf[h, pos], keys, values)
                part[i, :, 0, :, lanes] = dk.reshape(2, BLOCK, HEAD_SIZE)
                part[i, :, 1, :, lanes] = dv.reshape(2, BLOCK, HEAD_SIZE)
            return carry

        lax.fori_loop(0, spots(s), one, 0)

    def sum_send(d, r, s):
        return remote(
            sb.at[d, r, s], rb.at[d, r, s - 1], rs_s.at[d, r, s], rs_r.at[d, r, s - 1], ring[d]
        )

    def sum_land(d, r, s):
        return remote(
            sb.at[d, r, s], rb.at[d, r, s], rs_s.at[d, r, s], rs_r.at[d, r, s], ring[d]
        )

    def sum_slot(u, carry):
        s = half - u
        second_pass(s)
        for d in (0, 1):
            spot = 0 if d == 0 else jnp.where(s == half, 0, 1)
            for r in (0, 1):

                @pl.when(s == hops(d, r))
                def _():
                    sb[d, r, s] = part[spot, r].astype(BF16)

                @pl.when(s < hops(d, r))
                def _():
                    sum_land(d, r, s).wait_recv()
                    sb[d, r, s] = (part[spot, r] + rb[d, r, s].astype(F32)).astype(BF16)

                @pl.when(s <= hops(d, r))
                def _():
                    sum_send(d, r, s).start()

        return carry

    lax.fori_loop(0, half, sum_slot, 0)
    second_pass(0)

    def arrived(r):
        for d in (0, 1):
            sum_land(d, r, 0).wait_recv()
        return part[0, r] + rb[0, r, 0].astype(F32) + rb[1, r, 0].astype(F32)

    yb[0] = arrived(1).astype(BF16)
    cross = remote(yb.at[0], yb.at[1], y_s.at[1], y_r.at[1], ypart)
    cross.start()

    for h in range(HEADS):
        lanes = slice(h * 128, (h + 1) * 128)
        dk, dv = key_terms(h, sc[h], kvc[0, :, lanes], kvc[1, :, lanes])
        gkvc[0, :, lanes] = dk.astype(BF16)
        gkvc[1, :, lanes] = dv.astype(BF16)
        for j in range(GROUP):
            at = (h * GROUP + j) * HEAD_SIZE
            tile = (dq_t[h, :, j * BLOCK : (j + 1) * BLOCK].T * SCALE).astype(BF16)
            gqs[0, :, at : at + 128] = tile[:T]
            gqs[1, :, at : at + 128] = tile[T:]

    def give(i, src_own, src_sib, out, lanes):
        return (
            pltpu.make_async_copy(src_own, out.at[:, lanes], loc.at[i]),
            remote(src_sib, out.at[:, lanes], ret_s.at[i], ret_r.at[i], sib),
        )

    gives = [
        give(0, gqs.at[0], gqs.at[1], gq_out, own_q),
        give(1, gkvc.at[0, pl.ds(0, T)], gkvc.at[0, pl.ds(T, T)], gkc_out, own_k),
        give(2, gkvc.at[1, pl.ds(0, T)], gkvc.at[1, pl.ds(T, T)], gvc_out, own_k),
    ]
    for near, far in gives:
        near.start()
        far.start()

    sum0 = arrived(0)
    cross.wait_recv()
    sum0 = (sum0 + yb[1].astype(F32)).astype(BF16)
    dkb[z, 0] = sum0[0]
    dvf[...] = sum0[1]
    dk_across = gather_start(dkb, dk_s, dk_r, 2)
    late = [
        give(3, dkb.at[z, 0, own_rows], dkb.at[z, 0, sib_rows], gpk_out, own_k),
        give(4, dvf.at[own_rows], dvf.at[sib_rows], gpv_out, own_k),
    ]
    for near, far in late:
        near.start()
        far.start()
    copies[7].wait()
    lands[8].wait_recv()
    proj[...] = jnp.zeros(proj.shape, F32)

    def project(s):
        def one(i, carry):
            pos = lax.rem(z + n_z + (1 - 2 * i) * s, n_z)
            for r in (0, 1):
                row = ((y if r == 0 else 1 - y) * n_z + pos) * BLOCK
                rows = pl.ds(pl.multiple_of(row, BLOCK), BLOCK)
                keys_grad = dkb[pos, r].T
                for i_st in (0, 1):
                    proj[i_st] += dot(keys_grad, st[i_st, rows, :])
            return carry

        lax.fori_loop(0, spots(s), one, 0)

    gather_across(dkb, dk_s, dk_r, dk_across)

    def dk_slot(s, carry):
        @pl.when(s > 0)
        def _():
            gather_step(dkb, dk_s, dk_r, s)

        project(s)
        return carry

    lax.fori_loop(0, half + 1, dk_slot, 0)

    def proj_send(i_st, t):
        rows = pl.ds(pl.multiple_of(t * cols, cols), cols)
        return remote(
            proj.at[i_st, rows],
            prx.at[g],
            pj_s.at[i_st, t],
            pj_r.at[g],
            c if i_st == 0 else sib,
            core * per_core + t,
        )

    def scatter(t, carry):
        @pl.when(core * per_core + t != g)
        def _():
            proj_send(0, t).start()

        @pl.when(core * per_core + t == g)
        def _():
            rows = pl.ds(pl.multiple_of(t * cols, cols), cols)
            prx[g] = proj[0, rows]

        proj_send(1, t).start()
        return carry

    lax.fori_loop(0, per_core, scatter, 0)

    def collect(i, acc):
        @pl.when(jnp.logical_or(src_ctx != c, i != g))
        def _():
            remote(prx.at[i], prx.at[i], pj_s.at[0, 0], pj_r.at[i], sib).wait_recv()

        return acc + prx[i]

    gproj_out[...] = lax.fori_loop(0, n_dp, collect, jnp.zeros(gproj_out.shape, F32))

    def scatter_drain(t, carry):
        @pl.when(core * per_core + t != g)
        def _():
            proj_send(0, t).wait_send()

        proj_send(1, t).wait_send()
        return carry

    lax.fori_loop(0, per_core, scatter_drain, 0)
    for send in sends:
        send.wait_send()
    gather_drain(kvb, kv_s, kv_r, kv_across)
    gather_drain(dkb, dk_s, dk_r, dk_across)
    cross.wait_send()
    for d in (0, 1):
        for r in (0, 1):

            def drain(s, carry):
                sum_send(d, r, s).wait_send()
                return carry

            lax.fori_loop(1, hops(d, r) + 1, drain, 0)
    for near, far in gives + late:
        near.wait()
        far.wait()


def body(q, do, o, kc, vc, pk, pv, states, lengths):
    n_ctx = lax.axis_size("ctx")
    n_dp = lax.axis_size("dp")
    n_z = n_ctx // 4
    half = n_z // 2
    prompt = states.shape[1]
    width = states.shape[2]
    cols = KEY_HEAD_COUNT * HEAD_SIZE // n_dp
    hbm = pl.BlockSpec(memory_space=pl.ANY)
    dma = pltpu.SemaphoreType.DMA
    out = pl.pallas_call(
        functools.partial(kernel, n_z, n_dp),
        out_shape=[
            jax.ShapeDtypeStruct(q.shape[1:], BF16),
            jax.ShapeDtypeStruct(kc.shape[1:], BF16),
            jax.ShapeDtypeStruct(vc.shape[1:], BF16),
            jax.ShapeDtypeStruct(pk.shape[1:], BF16),
            jax.ShapeDtypeStruct(pv.shape[1:], BF16),
            jax.ShapeDtypeStruct((cols, width), F32),
        ],
        in_specs=[hbm] * 8 + [pl.BlockSpec(memory_space=pltpu.SMEM)],
        out_specs=[hbm] * 5 + [pl.BlockSpec(memory_space=pltpu.VMEM)],
        scratch_shapes=[
            pltpu.VMEM((n_z, 2, 2, BLOCK, KW), BF16),
            pltpu.VMEM((3, 2, T, QW), BF16),
            pltpu.VMEM((2, BLOCK, KW), BF16),
            pltpu.VMEM((T, BLOCK), BF16),
            pltpu.VMEM((BLOCK, BLOCK), BF16),
            pltpu.VMEM((2, prompt, width), BF16),
            pltpu.VMEM((HEADS, ROWS, HEAD_SIZE), BF16),
            pltpu.VMEM((HEADS, ROWS, HEAD_SIZE), BF16),
            pltpu.VMEM((HEADS, HEAD_SIZE, ROWS), BF16),
            pltpu.VMEM((HEADS, HEAD_SIZE, ROWS), BF16),
            pltpu.VMEM((HEADS, 1, ROWS), F32),
            pltpu.VMEM((HEADS, 1, ROWS), F32),
            pltpu.VMEM((HEADS, 1, ROWS), F32),
            pltpu.VMEM((HEADS, n_z, 2 * BLOCK, ROWS), F32),
            pltpu.VMEM((HEADS, BLOCK, ROWS), F32),
            pltpu.VMEM((HEADS, HEAD_SIZE, ROWS), F32),
            pltpu.VMEM((2, 2, 2, BLOCK, KW), F32),
            pltpu.VMEM((2, 2, half + 1, 2, BLOCK, KW), BF16),
            pltpu.VMEM((2, 2, half + 1, 2, BLOCK, KW), BF16),
            pltpu.VMEM((2, 2, BLOCK, KW), BF16),
            pltpu.VMEM((n_z, 2, BLOCK, KW), BF16),
            pltpu.VMEM((BLOCK, KW), BF16),
            pltpu.VMEM((2, KW, width), F32),
            pltpu.VMEM((n_dp, cols, width), F32),
            pltpu.VMEM((2, T, QW), BF16),
            pltpu.VMEM((2, BLOCK, KW), BF16),
            dma((8,)),
            dma((9,)),
            dma((9,)),
            dma((3,)),
            dma((3,)),
            dma((2, 2, half + 1)),
            dma((2, 2, half + 1)),
            dma((2, 2, half + 1)),
            dma((2, 2, half + 1)),
            dma((2, 2, half + 1)),
            dma((2, 2, half + 1)),
            dma((2, n_dp // 2)),
            dma((n_dp,)),
            dma((5,)),
            dma((5,)),
        ],
        compiler_params=pltpu.CompilerParams(
            collective_id=0, has_side_effects=True, vmem_limit_bytes=56 * 2**20
        ),
    )(q[0], do[0], o[0], kc[0], vc[0], pk[0], pv[0], states[0], lengths[0, 0])
    return (*(x[None] for x in out[:5]), out[5].T)


def solution(mesh):
    split = P("dp", "ctx", None)
    return jax.shard_map(
        body,
        mesh=mesh,
        in_specs=(split,) * 7 + (P("dp", None, "ctx"), split),
        out_specs=(split,) * 5 + (P("ctx", "dp"),),
        check_vma=False,
    )
```

```python
import functools
import math

import jax
import jax.numpy as jnp
from jax import lax
from jax.experimental import pallas as pl
from jax.experimental.pallas import tpu as pltpu
from jax.sharding import PartitionSpec as P

QUERY_HEAD_COUNT = 20
KEY_HEAD_COUNT = 4
HEAD_SIZE = 128
GROUP = QUERY_HEAD_COUNT // KEY_HEAD_COUNT
MASKED = -1e30
SCALE = HEAD_SIZE ** (-0.5)
LOG2E = math.log2(math.e)
MESH = pl.DeviceIdType.MESH
F32 = jnp.float32
BF16 = jnp.bfloat16

HEADS = KEY_HEAD_COUNT // 2
KW = HEADS * HEAD_SIZE
QW = HEADS * GROUP * HEAD_SIZE
T = 64
ROWS = GROUP * 2 * T
BLOCK = 2 * T


def dot(a, b, ca=1, cb=0):
    return lax.dot_general(a, b, (((ca,), (cb,)), ((), ())), preferred_element_type=F32)


def kernel(
    n_z,
    n_dp,
    q_in,
    do_in,
    o_in,
    kc_in,
    vc_in,
    pk_in,
    pv_in,
    st_in,
    len_in,
    gq_out,
    gkc_out,
    gvc_out,
    gpk_out,
    gpv_out,
    gproj_out,
    kb,
    vb,
    raw,
    kvc,
    bias_own,
    bias,
    st,
    qs,
    dos,
    q_t,
    do_t,
    delta,
    top,
    total,
    sbuf,
    sc,
    dq_t,
    part,
    sb,
    rb,
    yb,
    dkb,
    dvf,
    proj,
    pack,
    prx,
    gqs,
    gkvc,
    loc,
    sib_s,
    sib_r,
    y_s,
    y_r,
    k_s,
    k_r,
    v_s,
    v_r,
    rs_s,
    rs_r,
    dk_s,
    dk_r,
    pj_s,
    pj_r,
    ret_s,
    ret_r,
):
    half = n_z // 2
    per_core = n_dp // 2
    cols = KEY_HEAD_COUNT * HEAD_SIZE // n_dp
    width = st.shape[1]
    c = lax.axis_index("ctx")
    g = lax.axis_index("dp")
    core = lax.rem(c, 2)
    z = lax.rem(c // 2, n_z)
    y = c // (2 * n_z)
    base = y * (2 * n_z)
    sib = c + 1 - 2 * core
    ypart = (1 - y) * (2 * n_z) + z * 2 + core
    right = base + lax.rem(z + 1, n_z) * 2 + core
    left = base + lax.rem(z + n_z - 1, n_z) * 2 + core
    ring = (right, left)

    def remote(src, dst, s_sem, r_sem, ctx, dp=None):
        return pltpu.make_async_remote_copy(
            src_ref=src,
            dst_ref=dst,
            send_sem=s_sem,
            recv_sem=r_sem,
            device_id=(ctx, g if dp is None else dp),
            device_id_type=MESH,
        )

    def greet(ctx, dp):
        pl.semaphore_signal(
            pltpu.get_barrier_semaphore(), inc=1, device_id=(ctx, dp), device_id_type=MESH
        )

    for other in (sib, ypart, right, left):
        greet(other, g)
    src_core = g // per_core
    src_ctx = c - core + src_core

    def greet_source(i, carry):
        @pl.when(jnp.logical_or(src_ctx != c, i != g))
        def _():
            greet(src_ctx, i)

        return carry

    lax.fori_loop(0, n_dp, greet_source, 0)

    own_q = pl.ds(pl.multiple_of(core * QW, 128), QW)
    sib_q = pl.ds(pl.multiple_of((1 - core) * QW, 128), QW)
    own_k = pl.ds(pl.multiple_of(core * KW, 128), KW)
    sib_k = pl.ds(pl.multiple_of((1 - core) * KW, 128), KW)
    own_rows = pl.ds(pl.multiple_of(core * T, T), T)
    sib_rows = pl.ds(pl.multiple_of((1 - core) * T, T), T)
    def head_lanes(which, h):
        return pl.ds(pl.multiple_of(which * KW + h * HEAD_SIZE, 128), HEAD_SIZE)

    copies = [
        pltpu.make_async_copy(source.at[:, head_lanes(core, h)], buf.at[z, 0, h, own_rows], loc.at[i])
        for i, (source, buf, h) in enumerate(
            [(pk_in, kb, 0), (pk_in, kb, 1), (pv_in, vb, 0), (pv_in, vb, 1)]
        )
    ] + [
        pltpu.make_async_copy(q_in.at[:, own_q], raw.at[0, 0], loc.at[4]),
        pltpu.make_async_copy(do_in.at[:, own_q], raw.at[1, 0], loc.at[5]),
        pltpu.make_async_copy(o_in.at[:, own_q], raw.at[2, 0], loc.at[6]),
        pltpu.make_async_copy(kc_in.at[:, own_k], kvc.at[0, pl.ds(0, T)], loc.at[7]),
        pltpu.make_async_copy(vc_in.at[:, own_k], kvc.at[1, pl.ds(0, T)], loc.at[8]),
        pltpu.make_async_copy(st_in, st.at[0], loc.at[9]),
    ]
    for copy in copies:
        copy.start()

    key_at = lax.broadcasted_iota(jnp.int32, (T, 2 * T), 0)
    lane = lax.broadcasted_iota(jnp.int32, (T, 2 * T), 1)
    end0 = len_in[0]
    end1 = end0 + len_in[1]
    end2 = end1 + len_in[2]

    def slot(position):
        return (
            (position >= end0).astype(jnp.int32)
            + (position >= end1).astype(jnp.int32)
            + (position >= end2).astype(jnp.int32)
        )

    def shifted(offset):
        token = lane - offset
        seen = (token >= 0) & (token < T) & (key_at <= token) & (slot(key_at) == slot(token))
        return jnp.where(seen, 0.0, MASKED).astype(BF16)

    bias[0:T, :] = shifted(0)
    bias_own[...] = shifted(T)

    self_target = (src_core == core).astype(jnp.int32)
    pl.semaphore_wait(pltpu.get_barrier_semaphore(), 4 + n_dp - self_target)

    pairs = [
        (source.at[:, head_lanes(1 - core, h)], buf.at[z, 0, h, own_rows], buf.at[z, 0, h, sib_rows])
        for source, buf, h in [(pk_in, kb, 0), (pk_in, kb, 1), (pv_in, vb, 0), (pv_in, vb, 1)]
    ] + [
        (q_in.at[:, sib_q], raw.at[0, 1], raw.at[0, 1]),
        (do_in.at[:, sib_q], raw.at[1, 1], raw.at[1, 1]),
        (o_in.at[:, sib_q], raw.at[2, 1], raw.at[2, 1]),
        (kc_in.at[:, sib_k], kvc.at[0, pl.ds(T, T)], kvc.at[0, pl.ds(T, T)]),
        (vc_in.at[:, sib_k], kvc.at[1, pl.ds(T, T)], kvc.at[1, pl.ds(T, T)]),
        (st_in, st.at[1], st.at[1]),
        (bias_own, bias.at[pl.ds(T, T)], bias.at[pl.ds(T, T)]),
    ]
    sends = [
        remote(src, dst, sib_s.at[i], sib_r.at[i], sib) for i, (src, dst, _) in enumerate(pairs)
    ]
    lands = [
        remote(land, land, sib_s.at[i], sib_r.at[i], sib) for i, (_, _, land) in enumerate(pairs)
    ]
    for i in (0, 1, 2, 3, 4, 5, 6, 7, 8, 10, 9):
        sends[i].start()

    def hops(d, r):
        return half - r if d == 0 else half - 1 + r

    def place(d, s):
        return lax.rem(z + (n_z - s if d == 0 else s), n_z)

    def gather_send(buf, s_sem, r_sem, d, r, h, s):
        block = buf.at[place(d, s), r, h]
        return remote(block, block, s_sem.at[d, r, h, s + 1], r_sem.at[d, r, h, s + 1], ring[d])

    def gather_land(buf, s_sem, r_sem, d, r, h, s):
        block = buf.at[place(d, s), r, h]
        return remote(block, block, s_sem.at[d, r, h, s], r_sem.at[d, r, h, s], ring[d])

    def gather_start(buf, s_sem, r_sem, r, h):
        for d in (0, 1):
            gather_send(buf, s_sem, r_sem, d, r, h, 0).start()

    def across(src, dst, i):
        return remote(src, dst, y_s.at[i], y_r.at[i], ypart)

    def gather_step(buf, s_sem, r_sem, s, heads):
        for r in (0, 1):
            for h in heads:
                for d in (0, 1):

                    @pl.when(s <= hops(d, r))
                    def _():
                        gather_land(buf, s_sem, r_sem, d, r, h, s).wait_recv()

                    @pl.when(s < hops(d, r))
                    def _():
                        gather_send(buf, s_sem, r_sem, d, r, h, s).start()

    def gather_drain(buf, s_sem, r_sem):
        for d in (0, 1):
            for r in (0, 1):

                def drain(s, carry):
                    for h in range(HEADS):
                        gather_send(buf, s_sem, r_sem, d, r, h, s).wait_send()
                    return carry

                lax.fori_loop(0, hops(d, r), drain, 0)

    def spots(s):
        return jnp.where((s == 0) | (s == half), 1, 2)

    def landed(*which):
        for i in which:
            copies[i].wait()
            lands[i].wait_recv()

    keys, values = (kb, k_s, k_r), (vb, v_s, v_r)
    crossings = []
    for kind, chain in enumerate((keys, values)):
        for h in range(HEADS):
            landed(2 * kind + h)
            gather_start(*chain, 0, h)
            crossings.append(across(chain[0].at[z, 0, h], chain[0].at[z, 1, h], 2 * kind + h))
            crossings[-1].start()

    def tiles(i, h, j):
        at = (h * GROUP + j) * HEAD_SIZE
        return jnp.concatenate([raw[i, 0, :, at : at + 128], raw[i, 1, :, at : at + 128]], 0)

    landed(4)
    for h in range(HEADS):
        for j in range(GROUP):
            rows = slice(j * BLOCK, (j + 1) * BLOCK)
            q_tile = tiles(0, h, j)
            qs[h, rows, :] = q_tile
            q_t[h, :, rows] = q_tile.T

    def merge(h, scores):
        old = top[h]
        new = jnp.maximum(old, jnp.max(scores, axis=0, keepdims=True))
        total[h] = total[h] * jnp.exp2(old - new) + jnp.sum(
            jnp.exp2(scores - new), axis=0, keepdims=True
        )
        top[h] = new

    for h in range(HEADS):
        crossings[h].wait_recv()
        gather_start(*keys, 1, h)
    landed(7, 8)
    lands[10].wait_recv()
    mask_tile = bias[...].astype(F32)
    for h in range(HEADS):
        scores = dot(kvc[0, :, h * 128 : (h + 1) * 128], q_t[h]) * (SCALE * LOG2E)
        scores = scores + jnp.concatenate([mask_tile] * GROUP, axis=1)
        sc[h] = scores
        new = jnp.max(scores, axis=0, keepdims=True)
        top[h] = new
        total[h] = jnp.sum(jnp.exp2(scores - new), axis=0, keepdims=True)
        dq_t[h] = jnp.zeros((HEAD_SIZE, ROWS), F32)

    def first_pass(s):
        def one(i, carry):
            pos = lax.rem(z + n_z + (1 - 2 * i) * s, n_z)
            for h in range(HEADS):
                block = kb[pos, :, h].reshape(2 * BLOCK, HEAD_SIZE)
                scores = dot(block, q_t[h]) * (SCALE * LOG2E)
                sbuf[h, pos] = scores
                merge(h, scores)
            return carry

        lax.fori_loop(0, spots(s), one, 0)

    first_pass(0)
    for h in range(HEADS):
        crossings[2 + h].wait_recv()
        gather_start(*values, 1, h)
    landed(5, 6)
    for h in range(HEADS):
        for j in range(GROUP):
            rows = slice(j * BLOCK, (j + 1) * BLOCK)
            do_tile = tiles(1, h, j)
            dos[h, rows, :] = do_tile
            do_t[h, :, rows] = do_tile.T
            product = do_tile.astype(F32) * tiles(2, h, j).astype(F32)
            delta[h, :, rows] = jnp.sum(product.T, axis=0, keepdims=True)

    def gather_slot(s, carry):
        gather_step(*keys, s, range(HEADS))
        gather_step(*values, s, range(HEADS))
        first_pass(s)
        return carry

    lax.fori_loop(1, half + 1, gather_slot, 0)
    for h in range(HEADS):
        top[h] = top[h] + jnp.log2(total[h])

    def key_terms(h, scores, key_block, value_block):
        probs = jnp.exp2(scores - top[h])
        dprobs = dot(value_block, do_t[h])
        dscores = (probs * (dprobs - delta[h])).astype(BF16)
        dv = dot(probs.astype(BF16), dos[h])
        dk = dot(dscores, qs[h]) * SCALE
        dq_t[h] += dot(key_block, dscores, 0, 0)
        return dk, dv

    def second_pass(s):
        def one(i, carry):
            pos = lax.rem(z + n_z + (1 - 2 * i) * s, n_z)
            for h in range(HEADS):
                key_block = kb[pos, :, h].reshape(2 * BLOCK, HEAD_SIZE)
                value_block = vb[pos, :, h].reshape(2 * BLOCK, HEAD_SIZE)
                dk, dv = key_terms(h, sbuf[h, pos], key_block, value_block)
                part[0, pos, :, h] = dk.reshape(2, BLOCK, HEAD_SIZE)
                part[1, pos, :, h] = dv.reshape(2, BLOCK, HEAD_SIZE)
            return carry

        lax.fori_loop(0, spots(s), one, 0)

    def sum_send(kind, d, r, h, s):
        return remote(
            sb.at[kind, d, r, h, s],
            rb.at[kind, d, r, h, s - 1],
            rs_s.at[kind, d, r, h, s],
            rs_r.at[kind, d, r, h, s - 1],
            ring[d],
        )

    def sum_land(kind, d, r, h, s):
        block = rb.at[kind, d, r, h, s]
        return remote(block, block, rs_s.at[kind, d, r, h, s], rs_r.at[kind, d, r, h, s], ring[d])

    def own_term(kind, d, r, h, s):
        return part[kind, place(1 - d, s), r, h]

    def sum_step(kind, s):
        for r in (1, 0):
            for h in range(HEADS):
                for d in (0, 1):

                    @pl.when(s == hops(d, r))
                    def _():
                        sb[kind, d, r, h, s] = own_term(kind, d, r, h, s).astype(BF16)

                    @pl.when(s < hops(d, r))
                    def _():
                        sum_land(kind, d, r, h, s).wait_recv()
                        sb[kind, d, r, h, s] = (
                            own_term(kind, d, r, h, s) + rb[kind, d, r, h, s].astype(F32)
                        ).astype(BF16)

                    @pl.when(s <= hops(d, r))
                    def _():
                        sum_send(kind, d, r, h, s).start()

    def arrived(kind, r, h):
        for d in (0, 1):
            sum_land(kind, d, r, h, 0).wait_recv()
        return (
            part[kind, z, r, h] + rb[kind, 0, r, h, 0].astype(F32) + rb[kind, 1, r, h, 0].astype(F32)
        )

    def sum_slot(u, carry):
        s = half - u
        second_pass(s)
        sum_step(0, s)
        return carry

    lax.fori_loop(0, half, sum_slot, 0)
    second_pass(0)

    def swap(kind, r, h):
        yb[kind, r, h, 0] = arrived(kind, r, h).astype(BF16)
        i = 4 + (kind * 2 + r) * HEADS + h
        crossing = across(yb.at[kind, r, h, 0], yb.at[kind, 1 - r, h, 1], i)
        crossing.start()
        return crossing, across(yb.at[kind, r, h, 1], yb.at[kind, r, h, 1], 4 + (kind * 2 + 1 - r) * HEADS + h)

    swaps = {}
    for h in range(HEADS):
        for r in (1, 0):
            swaps[0, r, h] = swap(0, r, h)
    sum_step(1, half)

    for h in range(HEADS):
        lanes = slice(h * 128, (h + 1) * 128)
        dk, dv = key_terms(h, sc[h], kvc[0, :, lanes], kvc[1, :, lanes])
        gkvc[0, :, lanes] = dk.astype(BF16)
        gkvc[1, :, lanes] = dv.astype(BF16)

    for h in range(HEADS):
        for j in range(GROUP):
            at = (h * GROUP + j) * HEAD_SIZE
            tile = (dq_t[h, :, j * BLOCK : (j + 1) * BLOCK].T * SCALE).astype(BF16)
            gqs[0, :, at : at + 128] = tile[:T]
            gqs[1, :, at : at + 128] = tile[T:]

    def give(i, src_own, src_sib, out, lanes):
        return (
            pltpu.make_async_copy(src_own, out.at[:, lanes], loc.at[i]),
            remote(src_sib, out.at[:, lanes], ret_s.at[i], ret_r.at[i], sib),
        )

    gives = [
        give(0, gqs.at[0], gqs.at[1], gq_out, own_q),
        give(1, gkvc.at[0, pl.ds(0, T)], gkvc.at[0, pl.ds(T, T)], gkc_out, own_k),
        give(2, gkvc.at[1, pl.ds(0, T)], gkvc.at[1, pl.ds(T, T)], gvc_out, own_k),
    ]
    for near, far in gives:
        near.start()
        far.start()

    sum_step(1, half - 1)
    copies[9].wait()
    lands[9].wait_recv()
    proj[...] = jnp.zeros(proj.shape, F32)
    grads = (dkb, dk_s, dk_r)

    def finish(kind, r, h):
        swaps[kind, r, h][1].wait_recv()
        near_sum = part[kind, z, r, h] + rb[kind, 0, r, h, 0].astype(F32)
        near_sum = near_sum + rb[kind, 1, r, h, 0].astype(F32)
        return (near_sum + yb[kind, r, h, 1].astype(F32)).astype(BF16)

    def give_prompt(i, buf, out, h):
        lanes = head_lanes(core, h)
        gives.append(give(i, buf.at[own_rows], buf.at[sib_rows], out, lanes))
        for copy in gives[-1]:
            copy.start()

    for r in (0, 1):
        for h in range(HEADS):
            dkb[z, r, h] = finish(0, r, h)
            gather_start(*grads, r, h)
            if r == 0:
                give_prompt(3 + h, dkb.at[z, 0, h], gpk_out, h)

    def project(h, s):
        def one(i, carry):
            pos = lax.rem(z + n_z + (1 - 2 * i) * s, n_z)
            for r in (0, 1):
                row = ((y if r == 0 else 1 - y) * n_z + pos) * BLOCK
                rows = pl.ds(pl.multiple_of(row, BLOCK), BLOCK)
                states = st[:, :, rows].reshape(2 * width, BLOCK)
                proj[h] += dot(states, dkb[pos, r, h])
            return carry

        lax.fori_loop(0, spots(s), one, 0)

    def proj_send(i_st, t):
        return remote(
            pack.at[i_st, t],
            prx.at[g],
            pj_s.at[i_st, t],
            pj_r.at[g],
            c if i_st == 0 else sib,
            core * per_core + t,
        )

    quarter = cols // 4
    lanes_at = lax.broadcasted_iota(jnp.int32, (quarter, HEAD_SIZE), 1) // 32
    per_head = per_core // HEADS

    def scatter(h):
        for i_st in (0, 1):
            turned = proj[h, i_st * width : (i_st + 1) * width].T
            head = turned[:, :128]
            tail = jnp.concatenate([turned[:, 128:], jnp.zeros((HEAD_SIZE, 96), F32)], axis=1)
            for k in range(per_head):
                t = h * per_head + k
                pack[i_st, t, :cols] = head[k * cols : (k + 1) * cols]
                folded = jnp.zeros((quarter, 128), F32)
                for j in range(4):
                    at = k * cols + j * quarter
                    piece = tail[at : at + quarter]
                    if j:
                        piece = pltpu.roll(piece, 32 * j, 1)
                    folded = jnp.where(lanes_at == j, piece, folded)
                pack[i_st, t, cols:] = folded

                @pl.when(core * per_core + t + i_st * n_dp != g)
                def _():
                    proj_send(i_st, t).start()

    for h in range(HEADS):
        project(h, 0)
    for s in range(1, half):
        for h in range(HEADS):
            gather_step(*grads, s, (h,))
        for h in range(HEADS):
            project(h, s)
    for h in range(HEADS):
        gather_step(*grads, half, (h,))
        project(h, half)
        scatter(h)

    @pl.when(src_core == core)
    def _():
        prx[g] = pack[0, g - core * per_core]

    for s in range(half - 2, 0, -1):
        sum_step(1, s)
    for h in range(HEADS):
        yb[1, 1, h, 0] = arrived(1, 1, h).astype(BF16)
        i = 4 + 3 * HEADS + h
        crossing = across(yb.at[1, 1, h, 0], yb.at[1, 0, h, 1], i)
        crossing.start()
        swaps[1, 0, h] = (crossing, across(yb.at[1, 0, h, 1], yb.at[1, 0, h, 1], i))

    def collect(i, acc):
        @pl.when(jnp.logical_or(src_ctx != c, i != g))
        def _():
            remote(prx.at[i], prx.at[i], pj_s.at[0, 0], pj_r.at[i], sib).wait_recv()

        return acc + prx[i]

    summed = lax.fori_loop(0, n_dp, collect, jnp.zeros(prx.shape[1:], F32))
    gproj_out[:, :128] = summed[:cols]
    for j in range(4):
        piece = summed[cols:]
        if j:
            piece = pltpu.roll(piece, 128 - 32 * j, 1)
        gproj_out[j * quarter : (j + 1) * quarter, 128:] = piece[:, :32]

    for h in range(HEADS):
        arrived(1, 0, h)
        dvf[h] = finish(1, 0, h)
        give_prompt(3 + HEADS + h, dvf.at[h], gpv_out, h)

    def scatter_drain(t, carry):
        @pl.when(core * per_core + t != g)
        def _():
            proj_send(0, t).wait_send()

        proj_send(1, t).wait_send()
        return carry

    lax.fori_loop(0, per_core, scatter_drain, 0)
    for send in sends:
        send.wait_send()
    for chain in (keys, values, grads):
        gather_drain(*chain)
    for crossing in crossings:
        crossing.wait_send()
    for crossing, _ in swaps.values():
        crossing.wait_send()
    for kind in (0, 1):
        for d in (0, 1):
            for r in (0, 1):

                def drain(s, carry):
                    for h in range(HEADS):
                        sum_send(kind, d, r, h, s).wait_send()
                    return carry

                lax.fori_loop(1, hops(d, r) + 1, drain, 0)
    for near, far in gives:
        near.wait()
        far.wait()


def hand_on(*refs):
    count = len(refs) // 2
    for source, target in zip(refs[:count], refs[count:]):
        target[...] = source[...]


def body(q, do, o, kc, vc, pk, pv, states, lengths):
    n_ctx = lax.axis_size("ctx")
    n_dp = lax.axis_size("dp")
    n_z = n_ctx // 4
    half = n_z // 2
    prompt = states.shape[1]
    width = states.shape[2]
    cols = KEY_HEAD_COUNT * HEAD_SIZE // n_dp
    hbm = pl.BlockSpec(memory_space=pl.ANY)
    dma = pltpu.SemaphoreType.DMA
    out = pl.pallas_call(
        functools.partial(kernel, n_z, n_dp),
        out_shape=[
            jax.ShapeDtypeStruct(q.shape[1:], BF16),
            jax.ShapeDtypeStruct(kc.shape[1:], BF16),
            jax.ShapeDtypeStruct(vc.shape[1:], BF16),
            jax.ShapeDtypeStruct(pk.shape[1:], BF16),
            jax.ShapeDtypeStruct(pv.shape[1:], BF16),
            jax.ShapeDtypeStruct((cols, width), F32),
        ],
        in_specs=[hbm] * 8 + [pl.BlockSpec(memory_space=pltpu.SMEM)],
        out_specs=[hbm] * 5 + [pl.BlockSpec(memory_space=pltpu.VMEM)],
        scratch_shapes=[
            pltpu.VMEM((n_z, 2, HEADS, BLOCK, HEAD_SIZE), BF16),
            pltpu.VMEM((n_z, 2, HEADS, BLOCK, HEAD_SIZE), BF16),
            pltpu.VMEM((3, 2, T, QW), BF16),
            pltpu.VMEM((2, BLOCK, KW), BF16),
            pltpu.VMEM((T, BLOCK), BF16),
            pltpu.VMEM((BLOCK, BLOCK), BF16),
            pltpu.VMEM((2, width, prompt), BF16),
            pltpu.VMEM((HEADS, ROWS, HEAD_SIZE), BF16),
            pltpu.VMEM((HEADS, ROWS, HEAD_SIZE), BF16),
            pltpu.VMEM((HEADS, HEAD_SIZE, ROWS), BF16),
            pltpu.VMEM((HEADS, HEAD_SIZE, ROWS), BF16),
            pltpu.VMEM((HEADS, 1, ROWS), F32),
            pltpu.VMEM((HEADS, 1, ROWS), F32),
            pltpu.VMEM((HEADS, 1, ROWS), F32),
            pltpu.VMEM((HEADS, n_z, 2 * BLOCK, ROWS), F32),
            pltpu.VMEM((HEADS, BLOCK, ROWS), F32),
            pltpu.VMEM((HEADS, HEAD_SIZE, ROWS), F32),
            pltpu.VMEM((2, n_z, 2, HEADS, BLOCK, HEAD_SIZE), F32),
            pltpu.VMEM((2, 2, 2, HEADS, half + 1, BLOCK, HEAD_SIZE), BF16),
            pltpu.VMEM((2, 2, 2, HEADS, half + 1, BLOCK, HEAD_SIZE), BF16),
            pltpu.VMEM((2, 2, HEADS, 2, BLOCK, HEAD_SIZE), BF16),
            pltpu.VMEM((n_z, 2, HEADS, BLOCK, HEAD_SIZE), BF16),
            pltpu.VMEM((HEADS, BLOCK, HEAD_SIZE), BF16),
            pltpu.VMEM((HEADS, 2 * width, HEAD_SIZE), F32),
            pltpu.VMEM((2, n_dp // 2, cols + cols // 4, 128), F32),
            pltpu.VMEM((n_dp, cols + cols // 4, 128), F32),
            pltpu.VMEM((2, T, QW), BF16),
            pltpu.VMEM((2, BLOCK, KW), BF16),
            dma((10,)),
            dma((11,)),
            dma((11,)),
            dma((12,)),
            dma((12,)),
            *[dma((2, 2, HEADS, half + 1))] * 4,
            dma((2, 2, 2, HEADS, half + 1)),
            dma((2, 2, 2, HEADS, half + 1)),
            *[dma((2, 2, HEADS, half + 1))] * 2,
            dma((2, n_dp // 2)),
            dma((n_dp,)),
            dma((7,)),
            dma((7,)),
        ],
        compiler_params=pltpu.CompilerParams(
            collective_id=0, has_side_effects=True, vmem_limit_bytes=56 * 2**20
        ),
    )(q[0], do[0], o[0], kc[0], vc[0], pk[0], pv[0], states[0].T, lengths[0, 0])
    out = pl.pallas_call(
        hand_on,
        out_shape=[jax.ShapeDtypeStruct(x.shape, x.dtype) for x in out],
    )(*out)
    return (*(x[None] for x in out[:5]), out[5].T)


def solution(mesh):
    split = P("dp", "ctx", None)
    return jax.shard_map(
        body,
        mesh=mesh,
        in_specs=(split,) * 7 + (P("dp", None, "ctx"), split),
        out_specs=(split,) * 5 + (P("ctx", "dp"),),
        check_vma=False,
    )
```

```python
import functools
import math

import jax
import jax.numpy as jnp
from jax import lax
from jax.experimental import pallas as pl
from jax.experimental.pallas import tpu as pltpu
from jax.sharding import PartitionSpec as P

QUERY_HEAD_COUNT = 20
KEY_HEAD_COUNT = 4
HEAD_SIZE = 128
GROUP = QUERY_HEAD_COUNT // KEY_HEAD_COUNT
MASKED = -1e30
SCALE = HEAD_SIZE ** (-0.5)
LOG2E = math.log2(math.e)
MESH = pl.DeviceIdType.MESH
F32 = jnp.float32
BF16 = jnp.bfloat16

HEADS = KEY_HEAD_COUNT // 2
KW = HEADS * HEAD_SIZE
QW = HEADS * GROUP * HEAD_SIZE
T = 64
ROWS = GROUP * 2 * T
BLOCK = 2 * T


def dot(a, b, ca=1, cb=0):
    return lax.dot_general(a, b, (((ca,), (cb,)), ((), ())), preferred_element_type=F32)


def kernel(
    n_z,
    n_dp,
    q_in,
    do_in,
    o_in,
    kc_in,
    vc_in,
    pk_in,
    pv_in,
    st_in,
    len_in,
    gq_out,
    gkc_out,
    gvc_out,
    gpk_out,
    gpv_out,
    gproj_out,
    kb,
    vb,
    raw,
    kvc,
    bias_own,
    bias,
    st,
    qs,
    dos,
    q_t,
    do_t,
    delta,
    top,
    total,
    sbuf,
    sc,
    dq_t,
    part,
    sb,
    rb,
    yb,
    dkb,
    dvf,
    proj,
    pack,
    prx,
    gqs,
    gkvc,
    loc,
    sib_s,
    sib_r,
    y_s,
    y_r,
    k_s,
    k_r,
    v_s,
    v_r,
    rs_s,
    rs_r,
    dk_s,
    dk_r,
    pj_s,
    pj_r,
    ret_s,
    ret_r,
):
    half = n_z // 2
    per_core = n_dp // 2
    cols = KEY_HEAD_COUNT * HEAD_SIZE // n_dp
    width = st.shape[1]
    c = lax.axis_index("ctx")
    g = lax.axis_index("dp")
    core = lax.rem(c, 2)
    z = lax.rem(c // 2, n_z)
    y = c // (2 * n_z)
    base = y * (2 * n_z)
    sib = c + 1 - 2 * core
    ypart = (1 - y) * (2 * n_z) + z * 2 + core
    right = base + lax.rem(z + 1, n_z) * 2 + core
    left = base + lax.rem(z + n_z - 1, n_z) * 2 + core
    ring = (right, left)

    def remote(src, dst, s_sem, r_sem, ctx, dp=None):
        return pltpu.make_async_remote_copy(
            src_ref=src,
            dst_ref=dst,
            send_sem=s_sem,
            recv_sem=r_sem,
            device_id=(ctx, g if dp is None else dp),
            device_id_type=MESH,
        )

    def greet(ctx, dp):
        pl.semaphore_signal(
            pltpu.get_barrier_semaphore(), inc=1, device_id=(ctx, dp), device_id_type=MESH
        )

    for other in (sib, ypart, right, left):
        greet(other, g)
    src_core = g // per_core
    src_ctx = c - core + src_core

    def greet_source(i, carry):
        @pl.when(jnp.logical_or(src_ctx != c, i != g))
        def _():
            greet(src_ctx, i)

        return carry

    lax.fori_loop(0, n_dp, greet_source, 0)

    own_q = pl.ds(pl.multiple_of(core * QW, 128), QW)
    sib_q = pl.ds(pl.multiple_of((1 - core) * QW, 128), QW)
    own_k = pl.ds(pl.multiple_of(core * KW, 128), KW)
    sib_k = pl.ds(pl.multiple_of((1 - core) * KW, 128), KW)
    own_rows = pl.ds(pl.multiple_of(core * T, T), T)
    sib_rows = pl.ds(pl.multiple_of((1 - core) * T, T), T)
    def head_lanes(which, h):
        return pl.ds(pl.multiple_of(which * KW + h * HEAD_SIZE, 128), HEAD_SIZE)

    copies = [
        pltpu.make_async_copy(source.at[:, head_lanes(core, h)], buf.at[z, 0, h, own_rows], loc.at[i])
        for i, (source, buf, h) in enumerate(
            [(pk_in, kb, 0), (pk_in, kb, 1), (pv_in, vb, 0), (pv_in, vb, 1)]
        )
    ] + [
        pltpu.make_async_copy(q_in.at[:, own_q], raw.at[0, 0], loc.at[4]),
        pltpu.make_async_copy(do_in.at[:, own_q], raw.at[1, 0], loc.at[5]),
        pltpu.make_async_copy(o_in.at[:, own_q], raw.at[2, 0], loc.at[6]),
        pltpu.make_async_copy(kc_in.at[:, own_k], kvc.at[0, pl.ds(0, T)], loc.at[7]),
        pltpu.make_async_copy(vc_in.at[:, own_k], kvc.at[1, pl.ds(0, T)], loc.at[8]),
        pltpu.make_async_copy(st_in, st.at[0], loc.at[9]),
    ]
    for copy in copies:
        copy.start()

    key_at = lax.broadcasted_iota(jnp.int32, (T, 2 * T), 0)
    lane = lax.broadcasted_iota(jnp.int32, (T, 2 * T), 1)
    end0 = len_in[0]
    end1 = end0 + len_in[1]
    end2 = end1 + len_in[2]

    def slot(position):
        return (
            (position >= end0).astype(jnp.int32)
            + (position >= end1).astype(jnp.int32)
            + (position >= end2).astype(jnp.int32)
        )

    def shifted(offset):
        token = lane - offset
        seen = (token >= 0) & (token < T) & (key_at <= token) & (slot(key_at) == slot(token))
        return jnp.where(seen, 0.0, MASKED).astype(BF16)

    bias[0:T, :] = shifted(0)
    bias_own[...] = shifted(T)

    self_target = (src_core == core).astype(jnp.int32)
    pl.semaphore_wait(pltpu.get_barrier_semaphore(), 4 + n_dp - self_target)

    pairs = [
        (source.at[:, head_lanes(1 - core, h)], buf.at[z, 0, h, own_rows], buf.at[z, 0, h, sib_rows])
        for source, buf, h in [(pk_in, kb, 0), (pk_in, kb, 1), (pv_in, vb, 0), (pv_in, vb, 1)]
    ] + [
        (q_in.at[:, sib_q], raw.at[0, 1], raw.at[0, 1]),
        (do_in.at[:, sib_q], raw.at[1, 1], raw.at[1, 1]),
        (o_in.at[:, sib_q], raw.at[2, 1], raw.at[2, 1]),
        (kc_in.at[:, sib_k], kvc.at[0, pl.ds(T, T)], kvc.at[0, pl.ds(T, T)]),
        (vc_in.at[:, sib_k], kvc.at[1, pl.ds(T, T)], kvc.at[1, pl.ds(T, T)]),
        (st_in, st.at[1], st.at[1]),
        (bias_own, bias.at[pl.ds(T, T)], bias.at[pl.ds(T, T)]),
    ]
    sends = [
        remote(src, dst, sib_s.at[i], sib_r.at[i], sib) for i, (src, dst, _) in enumerate(pairs)
    ]
    lands = [
        remote(land, land, sib_s.at[i], sib_r.at[i], sib) for i, (_, _, land) in enumerate(pairs)
    ]
    for i in range(4):
        sends[i].start()

    def hops(d, r):
        return half - r if d == 0 else half - 1 + r

    def place(d, s):
        return lax.rem(z + (n_z - s if d == 0 else s), n_z)

    def gather_send(buf, s_sem, r_sem, d, r, h, s):
        block = buf.at[place(d, s), r, h]
        return remote(block, block, s_sem.at[d, r, h, s + 1], r_sem.at[d, r, h, s + 1], ring[d])

    def gather_land(buf, s_sem, r_sem, d, r, h, s):
        block = buf.at[place(d, s), r, h]
        return remote(block, block, s_sem.at[d, r, h, s], r_sem.at[d, r, h, s], ring[d])

    def gather_start(buf, s_sem, r_sem, r, h):
        for d in (0, 1):
            gather_send(buf, s_sem, r_sem, d, r, h, 0).start()

    def across(src, dst, i):
        return remote(src, dst, y_s.at[i], y_r.at[i], ypart)

    def gather_step(buf, s_sem, r_sem, r, s, heads=range(HEADS)):
        for h in heads:
            for d in (0, 1):

                @pl.when((s >= 1) & (s <= hops(d, r)))
                def _():
                    gather_land(buf, s_sem, r_sem, d, r, h, s).wait_recv()

                @pl.when((s >= 1) & (s < hops(d, r)))
                def _():
                    gather_send(buf, s_sem, r_sem, d, r, h, s).start()

    def gather_drain(buf, s_sem, r_sem):
        for d in (0, 1):
            for r in (0, 1):

                def drain(s, carry):
                    for h in range(HEADS):
                        gather_send(buf, s_sem, r_sem, d, r, h, s).wait_send()
                    return carry

                lax.fori_loop(0, hops(d, r), drain, 0)

    def spots(s):
        return jnp.where((s == 0) | (s == half), 1, 2)

    def landed(*which):
        for i in which:
            copies[i].wait()
            lands[i].wait_recv()

    keys, values = (kb, k_s, k_r), (vb, v_s, v_r)
    crossings = [
        across(buf.at[z, 0, h], buf.at[z, 1, h], 2 * kind + h)
        for kind, buf in enumerate((kb, vb))
        for h in range(HEADS)
    ]
    for h in range(HEADS):
        landed(h)
        gather_start(*keys, 0, h)
        crossings[h].start()
    for i in (4, 7, 8, 10, 5, 6, 9):
        sends[i].start()
    for h in range(HEADS):
        landed(2 + h)
        crossings[2 + h].start()
        gather_start(*values, 0, h)

    def tiles(i, h, j):
        at = (h * GROUP + j) * HEAD_SIZE
        return jnp.concatenate([raw[i, 0, :, at : at + 128], raw[i, 1, :, at : at + 128]], 0)

    landed(4)
    for h in range(HEADS):
        for j in range(GROUP):
            rows = slice(j * BLOCK, (j + 1) * BLOCK)
            q_tile = tiles(0, h, j)
            qs[h, rows, :] = q_tile
            q_t[h, :, rows] = q_tile.T

    def merge(h, scores):
        old = top[h]
        new = jnp.maximum(old, jnp.max(scores, axis=0, keepdims=True))
        total[h] = total[h] * jnp.exp2(old - new) + jnp.sum(
            jnp.exp2(scores - new), axis=0, keepdims=True
        )
        top[h] = new

    landed(7, 8)
    lands[10].wait_recv()
    mask_tile = bias[...].astype(F32)
    for h in range(HEADS):
        scores = dot(kvc[0, :, h * 128 : (h + 1) * 128], q_t[h]) * (SCALE * LOG2E)
        scores = scores + jnp.concatenate([mask_tile] * GROUP, axis=1)
        sc[h] = scores
        new = jnp.max(scores, axis=0, keepdims=True)
        top[h] = new
        total[h] = jnp.sum(jnp.exp2(scores - new), axis=0, keepdims=True)
        dq_t[h] = jnp.zeros((HEAD_SIZE, ROWS), F32)

    def first_pass(s):
        def one(i, carry):
            pos = lax.rem(z + n_z + (1 - 2 * i) * s, n_z)
            for h in range(HEADS):
                block = kb[pos, :, h].reshape(2 * BLOCK, HEAD_SIZE)
                scores = dot(block, q_t[h]) * (SCALE * LOG2E)
                sbuf[h, pos] = scores
                merge(h, scores)
            return carry

        lax.fori_loop(0, spots(s), one, 0)

    landed(5, 6)
    for h in range(HEADS):
        for j in range(GROUP):
            rows = slice(j * BLOCK, (j + 1) * BLOCK)
            do_tile = tiles(1, h, j)
            dos[h, rows, :] = do_tile
            do_t[h, :, rows] = do_tile.T
            product = do_tile.astype(F32) * tiles(2, h, j).astype(F32)
            delta[h, :, rows] = jnp.sum(product.T, axis=0, keepdims=True)

    def gather_slot(i, carry):
        gather_step(*keys, 0, i)
        gather_step(*values, 0, i)
        for lag, chain in ((1, keys), (2, values)):

            @pl.when(i == lag)
            def _():
                for h in range(HEADS):
                    crossings[2 * lag - 2 + h].wait_recv()
                    gather_start(*chain, 1, h)

            gather_step(*chain, 1, i - lag)

        @pl.when(i <= half + 1)
        def _():
            first_pass(i - 1)

        return carry

    lax.fori_loop(1, half + 3, gather_slot, 0)
    for h in range(HEADS):
        top[h] = top[h] + jnp.log2(total[h])

    def key_terms(h, scores, key_block, value_block):
        probs = jnp.exp2(scores - top[h])
        dprobs = dot(value_block, do_t[h])
        dscores = (probs * (dprobs - delta[h])).astype(BF16)
        dv = dot(probs.astype(BF16), dos[h])
        dk = dot(dscores, qs[h]) * SCALE
        dq_t[h] += dot(key_block, dscores, 0, 0)
        return dk, dv

    def second_pass(s, h):
        def one(i, carry):
            pos = lax.rem(z + n_z + (1 - 2 * i) * s, n_z)
            key_block = kb[pos, :, h].reshape(2 * BLOCK, HEAD_SIZE)
            value_block = vb[pos, :, h].reshape(2 * BLOCK, HEAD_SIZE)
            dk, dv = key_terms(h, sbuf[h, pos], key_block, value_block)
            part[0, pos, :, h] = dk.reshape(2, BLOCK, HEAD_SIZE)
            part[1, pos, :, h] = dv.reshape(2, BLOCK, HEAD_SIZE)
            return carry

        lax.fori_loop(0, spots(s), one, 0)

    def sum_send(kind, d, r, h, s):
        return remote(
            sb.at[kind, d, r, h, s],
            rb.at[kind, d, r, h, s - 1],
            rs_s.at[kind, d, r, h, s],
            rs_r.at[kind, d, r, h, s - 1],
            ring[d],
        )

    def sum_land(kind, d, r, h, s):
        block = rb.at[kind, d, r, h, s]
        return remote(block, block, rs_s.at[kind, d, r, h, s], rs_r.at[kind, d, r, h, s], ring[d])

    def own_term(kind, d, r, h, s):
        return part[kind, place(1 - d, s), r, h]

    long_set = ((0, 0), (1, 1))
    short_set = ((1, 0), (0, 1))

    def sum_step(kind, pairs, s, first=False, heads=range(HEADS)):
        for h in heads:
            for d, r in pairs:
                term = own_term(kind, d, r, h, s)
                if not first:
                    sum_land(kind, d, r, h, s).wait_recv()
                    term = term + rb[kind, d, r, h, s].astype(F32)
                sb[kind, d, r, h, s] = term.astype(BF16)
                sum_send(kind, d, r, h, s).start()

    def arrived(kind, r, h):
        for d in (0, 1):
            sum_land(kind, d, r, h, 0).wait_recv()
        return (
            part[kind, z, r, h] + rb[kind, 0, r, h, 0].astype(F32) + rb[kind, 1, r, h, 0].astype(F32)
        )

    def sum_slot(u, carry):
        s = half - u
        for h in range(HEADS):
            second_pass(s, h)

            @pl.when(u == 0)
            def _():
                sum_step(0, long_set, s, True, (h,))

            @pl.when(u == 1)
            def _():
                sum_step(0, short_set, s, True, (h,))

            @pl.when((u > 1) & (s > 0))
            def _():
                sum_step(0, short_set, s, False, (h,))

        @pl.when((u > 0) & (s > 0))
        def _():
            sum_step(0, long_set, s)

        return carry

    lax.fori_loop(0, half + 1, sum_slot, 0)

    def swap(kind, r, h):
        yb[kind, r, h, 0] = arrived(kind, r, h).astype(BF16)
        i = 4 + (kind * 2 + r) * HEADS + h
        crossing = across(yb.at[kind, r, h, 0], yb.at[kind, 1 - r, h, 1], i)
        crossing.start()
        return crossing, across(yb.at[kind, r, h, 1], yb.at[kind, r, h, 1], 4 + (kind * 2 + 1 - r) * HEADS + h)

    swaps = {}
    for h in range(HEADS):
        swaps[0, 1, h] = swap(0, 1, h)
    sum_step(1, long_set, half, True)

    for h in range(HEADS):
        lanes = slice(h * 128, (h + 1) * 128)
        dk, dv = key_terms(h, sc[h], kvc[0, :, lanes], kvc[1, :, lanes])
        gkvc[0, :, lanes] = dk.astype(BF16)
        gkvc[1, :, lanes] = dv.astype(BF16)

    sum_step(1, short_set, half - 1, True)
    for h in range(HEADS):
        swaps[0, 0, h] = swap(0, 0, h)

    for h in range(HEADS):
        for j in range(GROUP):
            at = (h * GROUP + j) * HEAD_SIZE
            tile = (dq_t[h, :, j * BLOCK : (j + 1) * BLOCK].T * SCALE).astype(BF16)
            gqs[0, :, at : at + 128] = tile[:T]
            gqs[1, :, at : at + 128] = tile[T:]

    def give(i, src_own, src_sib, out, lanes):
        return (
            pltpu.make_async_copy(src_own, out.at[:, lanes], loc.at[i]),
            remote(src_sib, out.at[:, lanes], ret_s.at[i], ret_r.at[i], sib),
        )

    gives = [
        give(0, gqs.at[0], gqs.at[1], gq_out, own_q),
        give(1, gkvc.at[0, pl.ds(0, T)], gkvc.at[0, pl.ds(T, T)], gkc_out, own_k),
        give(2, gkvc.at[1, pl.ds(0, T)], gkvc.at[1, pl.ds(T, T)], gvc_out, own_k),
    ]
    for near, far in gives:
        near.start()
        far.start()

    sum_step(1, long_set, half - 1)
    copies[9].wait()
    lands[9].wait_recv()
    proj[...] = jnp.zeros(proj.shape, F32)
    grads = (dkb, dk_s, dk_r)

    def finish(kind, r, h):
        swaps[kind, r, h][1].wait_recv()
        near_sum = part[kind, z, r, h] + rb[kind, 0, r, h, 0].astype(F32)
        near_sum = near_sum + rb[kind, 1, r, h, 0].astype(F32)
        return (near_sum + yb[kind, r, h, 1].astype(F32)).astype(BF16)

    def give_prompt(i, buf, out, h):
        lanes = head_lanes(core, h)
        gives.append(give(i, buf.at[own_rows], buf.at[sib_rows], out, lanes))
        for copy in gives[-1]:
            copy.start()

    for r in (0, 1):
        for h in range(HEADS):
            dkb[z, r, h] = finish(0, r, h)
            gather_start(*grads, r, h)
            if r == 0:
                give_prompt(3 + h, dkb.at[z, 0, h], gpk_out, h)
        if r == 0:
            sum_step(1, short_set, half - 2)

    def project(h, s):
        def one(i, carry):
            pos = lax.rem(z + n_z + (1 - 2 * i) * s, n_z)
            for r in (0, 1):
                row = ((y if r == 0 else 1 - y) * n_z + pos) * BLOCK
                rows = pl.ds(pl.multiple_of(row, BLOCK), BLOCK)
                states = st[:, :, rows].reshape(2 * width, BLOCK)
                proj[h] += dot(states, dkb[pos, r, h])
            return carry

        lax.fori_loop(0, spots(s), one, 0)

    def proj_send(i_st, t):
        return remote(
            pack.at[i_st, t],
            prx.at[g],
            pj_s.at[i_st, t],
            pj_r.at[g],
            c if i_st == 0 else sib,
            core * per_core + t,
        )

    quarter = cols // 4
    lanes_at = lax.broadcasted_iota(jnp.int32, (quarter, HEAD_SIZE), 1) // 32
    per_head = per_core // HEADS

    def scatter(h):
        for i_st in (0, 1):
            turned = proj[h, i_st * width : (i_st + 1) * width].T
            head = turned[:, :128]
            tail = jnp.concatenate([turned[:, 128:], jnp.zeros((HEAD_SIZE, 96), F32)], axis=1)
            for k in range(per_head):
                t = h * per_head + k
                pack[i_st, t, :cols] = head[k * cols : (k + 1) * cols]
                folded = jnp.zeros((quarter, 128), F32)
                for j in range(4):
                    at = k * cols + j * quarter
                    piece = tail[at : at + quarter]
                    if j:
                        piece = pltpu.roll(piece, 32 * j, 1)
                    folded = jnp.where(lanes_at == j, piece, folded)
                pack[i_st, t, cols:] = folded

                @pl.when(core * per_core + t + i_st * n_dp != g)
                def _():
                    proj_send(i_st, t).start()

    def value_final():
        for h in range(HEADS):
            yb[1, 1, h, 0] = arrived(1, 1, h).astype(BF16)
            i = 4 + 3 * HEADS + h
            crossing = across(yb.at[1, 1, h, 0], yb.at[1, 0, h, 1], i)
            crossing.start()
            swaps[1, 0, h] = (crossing, across(yb.at[1, 0, h, 1], yb.at[1, 0, h, 1], i))

    rest = []
    for s in range(half - 2, 0, -1):
        rest.append((long_set, s))
        if s > 1:
            rest.append((short_set, s - 1))
    when = {0: (), 1: rest[:1], 2: rest[1:], 3: ()} if half > 3 else {half - 1: rest}

    for h in range(HEADS):
        project(h, 0)
    for s in range(1, half):
        gather_step(*grads, 0, s)
        gather_step(*grads, 1, s)
        for pairs, at in when.get(s, ()):
            sum_step(1, pairs, at)
        if s == half - 1:
            value_final()
        for h in range(HEADS):
            project(h, s)
    for h in range(HEADS):
        for r in (0, 1):
            gather_step(*grads, r, half, (h,))
        project(h, half)
        scatter(h)

    @pl.when(src_core == core)
    def _():
        prx[g] = pack[0, g - core * per_core]

    def collect(i, acc):
        @pl.when(jnp.logical_or(src_ctx != c, i != g))
        def _():
            remote(prx.at[i], prx.at[i], pj_s.at[0, 0], pj_r.at[i], sib).wait_recv()

        return acc + prx[i]

    summed = lax.fori_loop(0, n_dp, collect, jnp.zeros(prx.shape[1:], F32))
    gproj_out[:, :128] = summed[:cols]
    for j in range(4):
        piece = summed[cols:]
        if j:
            piece = pltpu.roll(piece, 128 - 32 * j, 1)
        gproj_out[j * quarter : (j + 1) * quarter, 128:] = piece[:, :32]

    for h in range(HEADS):
        arrived(1, 0, h)
        dvf[h] = finish(1, 0, h)
        give_prompt(3 + HEADS + h, dvf.at[h], gpv_out, h)

    def scatter_drain(t, carry):
        @pl.when(core * per_core + t != g)
        def _():
            proj_send(0, t).wait_send()

        proj_send(1, t).wait_send()
        return carry

    lax.fori_loop(0, per_core, scatter_drain, 0)
    for send in sends:
        send.wait_send()
    for chain in (keys, values, grads):
        gather_drain(*chain)
    for crossing in crossings:
        crossing.wait_send()
    for crossing, _ in swaps.values():
        crossing.wait_send()
    for kind in (0, 1):
        for d in (0, 1):
            for r in (0, 1):

                def drain(s, carry):
                    for h in range(HEADS):
                        sum_send(kind, d, r, h, s).wait_send()
                    return carry

                lax.fori_loop(1, hops(d, r) + 1, drain, 0)
    for near, far in gives:
        near.wait()
        far.wait()


def hand_on(*refs):
    count = len(refs) // 2
    for source, target in zip(refs[:count], refs[count:]):
        target[...] = source[...]


def body(q, do, o, kc, vc, pk, pv, states, lengths):
    n_ctx = lax.axis_size("ctx")
    n_dp = lax.axis_size("dp")
    n_z = n_ctx // 4
    half = n_z // 2
    prompt = states.shape[1]
    width = states.shape[2]
    cols = KEY_HEAD_COUNT * HEAD_SIZE // n_dp
    hbm = pl.BlockSpec(memory_space=pl.ANY)
    dma = pltpu.SemaphoreType.DMA
    out = pl.pallas_call(
        functools.partial(kernel, n_z, n_dp),
        out_shape=[
            jax.ShapeDtypeStruct(q.shape[1:], BF16),
            jax.ShapeDtypeStruct(kc.shape[1:], BF16),
            jax.ShapeDtypeStruct(vc.shape[1:], BF16),
            jax.ShapeDtypeStruct(pk.shape[1:], BF16),
            jax.ShapeDtypeStruct(pv.shape[1:], BF16),
            jax.ShapeDtypeStruct((cols, width), F32),
        ],
        in_specs=[hbm] * 8 + [pl.BlockSpec(memory_space=pltpu.SMEM)],
        out_specs=[hbm] * 5 + [pl.BlockSpec(memory_space=pltpu.VMEM)],
        scratch_shapes=[
            pltpu.VMEM((n_z, 2, HEADS, BLOCK, HEAD_SIZE), BF16),
            pltpu.VMEM((n_z, 2, HEADS, BLOCK, HEAD_SIZE), BF16),
            pltpu.VMEM((3, 2, T, QW), BF16),
            pltpu.VMEM((2, BLOCK, KW), BF16),
            pltpu.VMEM((T, BLOCK), BF16),
            pltpu.VMEM((BLOCK, BLOCK), BF16),
            pltpu.VMEM((2, width, prompt), BF16),
            pltpu.VMEM((HEADS, ROWS, HEAD_SIZE), BF16),
            pltpu.VMEM((HEADS, ROWS, HEAD_SIZE), BF16),
            pltpu.VMEM((HEADS, HEAD_SIZE, ROWS), BF16),
            pltpu.VMEM((HEADS, HEAD_SIZE, ROWS), BF16),
            pltpu.VMEM((HEADS, 1, ROWS), F32),
            pltpu.VMEM((HEADS, 1, ROWS), F32),
            pltpu.VMEM((HEADS, 1, ROWS), F32),
            pltpu.VMEM((HEADS, n_z, 2 * BLOCK, ROWS), F32),
            pltpu.VMEM((HEADS, BLOCK, ROWS), F32),
            pltpu.VMEM((HEADS, HEAD_SIZE, ROWS), F32),
            pltpu.VMEM((2, n_z, 2, HEADS, BLOCK, HEAD_SIZE), F32),
            pltpu.VMEM((2, 2, 2, HEADS, half + 1, BLOCK, HEAD_SIZE), BF16),
            pltpu.VMEM((2, 2, 2, HEADS, half + 1, BLOCK, HEAD_SIZE), BF16),
            pltpu.VMEM((2, 2, HEADS, 2, BLOCK, HEAD_SIZE), BF16),
            pltpu.VMEM((n_z, 2, HEADS, BLOCK, HEAD_SIZE), BF16),
            pltpu.VMEM((HEADS, BLOCK, HEAD_SIZE), BF16),
            pltpu.VMEM((HEADS, 2 * width, HEAD_SIZE), F32),
            pltpu.VMEM((2, n_dp // 2, cols + cols // 4, 128), F32),
            pltpu.VMEM((n_dp, cols + cols // 4, 128), F32),
            pltpu.VMEM((2, T, QW), BF16),
            pltpu.VMEM((2, BLOCK, KW), BF16),
            dma((10,)),
            dma((11,)),
            dma((11,)),
            dma((12,)),
            dma((12,)),
            *[dma((2, 2, HEADS, half + 1))] * 4,
            dma((2, 2, 2, HEADS, half + 1)),
            dma((2, 2, 2, HEADS, half + 1)),
            *[dma((2, 2, HEADS, half + 1))] * 2,
            dma((2, n_dp // 2)),
            dma((n_dp,)),
            dma((7,)),
            dma((7,)),
        ],
        compiler_params=pltpu.CompilerParams(
            collective_id=0, has_side_effects=True, vmem_limit_bytes=56 * 2**20
        ),
    )(q[0], do[0], o[0], kc[0], vc[0], pk[0], pv[0], states[0].T, lengths[0, 0])
    out = pl.pallas_call(
        hand_on,
        out_shape=[jax.ShapeDtypeStruct(x.shape, x.dtype) for x in out],
    )(*out)
    return (*(x[None] for x in out[:5]), out[5].T)


def solution(mesh):
    split = P("dp", "ctx", None)
    return jax.shard_map(
        body,
        mesh=mesh,
        in_specs=(split,) * 7 + (P("dp", None, "ctx"), split),
        out_specs=(split,) * 5 + (P("ctx", "dp"),),
        check_vma=False,
    )
```

```python
import functools
import math

import jax
import jax.numpy as jnp
from jax import lax
from jax.experimental import pallas as pl
from jax.experimental.pallas import tpu as pltpu
from jax.sharding import PartitionSpec as P

QUERY_HEAD_COUNT = 20
KEY_HEAD_COUNT = 4
HEAD_SIZE = 128
GROUP = QUERY_HEAD_COUNT // KEY_HEAD_COUNT
MASKED = -1e30
SCALE = HEAD_SIZE ** (-0.5)
LOG2E = math.log2(math.e)
MESH = pl.DeviceIdType.MESH
F32 = jnp.float32
BF16 = jnp.bfloat16

HEADS = KEY_HEAD_COUNT // 2
KW = HEADS * HEAD_SIZE
QW = HEADS * GROUP * HEAD_SIZE
T = 64
ROWS = GROUP * 2 * T
BLOCK = 2 * T


def dot(a, b, ca=1, cb=0):
    return lax.dot_general(a, b, (((ca,), (cb,)), ((), ())), preferred_element_type=F32)


def kernel(
    n_z,
    n_dp,
    q_in,
    do_in,
    o_in,
    kc_in,
    vc_in,
    pk_in,
    pv_in,
    st_in,
    len_in,
    gq_out,
    gkc_out,
    gvc_out,
    gpk_out,
    gpv_out,
    gproj_out,
    kb,
    vb,
    raw,
    kvc,
    bias_own,
    bias,
    st,
    qs,
    dos,
    q_t,
    do_t,
    delta,
    top,
    total,
    sbuf,
    sc,
    dq_t,
    part,
    sb,
    rb,
    yb,
    dkb,
    dvf,
    proj,
    pack,
    prx,
    gqs,
    gkvc,
    loc,
    sib_s,
    sib_r,
    y_s,
    y_r,
    k_s,
    k_r,
    v_s,
    v_r,
    rs_s,
    rs_r,
    dk_s,
    dk_r,
    pj_s,
    pj_r,
    ret_s,
    ret_r,
):
    half = n_z // 2
    per_core = n_dp // 2
    cols = KEY_HEAD_COUNT * HEAD_SIZE // n_dp
    width = st.shape[1]
    c = lax.axis_index("ctx")
    g = lax.axis_index("dp")
    core = lax.rem(c, 2)
    z = lax.rem(c // 2, n_z)
    y = c // (2 * n_z)
    base = y * (2 * n_z)
    sib = c + 1 - 2 * core
    ypart = (1 - y) * (2 * n_z) + z * 2 + core
    right = base + lax.rem(z + 1, n_z) * 2 + core
    left = base + lax.rem(z + n_z - 1, n_z) * 2 + core
    ring = (right, left)

    def remote(src, dst, s_sem, r_sem, ctx, dp=None):
        return pltpu.make_async_remote_copy(
            src_ref=src,
            dst_ref=dst,
            send_sem=s_sem,
            recv_sem=r_sem,
            device_id=(ctx, g if dp is None else dp),
            device_id_type=MESH,
        )

    def greet(ctx, dp):
        pl.semaphore_signal(
            pltpu.get_barrier_semaphore(), inc=1, device_id=(ctx, dp), device_id_type=MESH
        )

    for other in (sib, ypart, right, left):
        greet(other, g)
    src_core = g // per_core
    src_ctx = c - core + src_core

    def greet_source(i, carry):
        @pl.when(jnp.logical_or(src_ctx != c, i != g))
        def _():
            greet(src_ctx, i)

        return carry

    lax.fori_loop(0, n_dp, greet_source, 0)

    own_q = pl.ds(pl.multiple_of(core * QW, 128), QW)
    sib_q = pl.ds(pl.multiple_of((1 - core) * QW, 128), QW)
    own_k = pl.ds(pl.multiple_of(core * KW, 128), KW)
    sib_k = pl.ds(pl.multiple_of((1 - core) * KW, 128), KW)
    own_rows = pl.ds(pl.multiple_of(core * T, T), T)
    sib_rows = pl.ds(pl.multiple_of((1 - core) * T, T), T)
    def head_lanes(which, h):
        return pl.ds(pl.multiple_of(which * KW + h * HEAD_SIZE, 128), HEAD_SIZE)

    copies = [
        pltpu.make_async_copy(source.at[:, head_lanes(core, h)], buf.at[z, 0, h, own_rows], loc.at[i])
        for i, (source, buf, h) in enumerate(
            [(pk_in, kb, 0), (pk_in, kb, 1), (pv_in, vb, 0), (pv_in, vb, 1)]
        )
    ] + [
        pltpu.make_async_copy(q_in.at[:, own_q], raw.at[0, 0], loc.at[4]),
        pltpu.make_async_copy(do_in.at[:, own_q], raw.at[1, 0], loc.at[5]),
        pltpu.make_async_copy(o_in.at[:, own_q], raw.at[2, 0], loc.at[6]),
        pltpu.make_async_copy(kc_in.at[:, own_k], kvc.at[0, pl.ds(0, T)], loc.at[7]),
        pltpu.make_async_copy(vc_in.at[:, own_k], kvc.at[1, pl.ds(0, T)], loc.at[8]),
        pltpu.make_async_copy(st_in, st.at[0], loc.at[9]),
    ]
    for copy in copies:
        copy.start()

    key_at = lax.broadcasted_iota(jnp.int32, (T, 2 * T), 0)
    lane = lax.broadcasted_iota(jnp.int32, (T, 2 * T), 1)
    end0 = len_in[0]
    end1 = end0 + len_in[1]
    end2 = end1 + len_in[2]

    def slot(position):
        return (
            (position >= end0).astype(jnp.int32)
            + (position >= end1).astype(jnp.int32)
            + (position >= end2).astype(jnp.int32)
        )

    def shifted(offset):
        token = lane - offset
        seen = (token >= 0) & (token < T) & (key_at <= token) & (slot(key_at) == slot(token))
        return jnp.where(seen, 0.0, MASKED).astype(BF16)

    bias[0:T, :] = shifted(0)
    bias_own[...] = shifted(T)

    self_target = (src_core == core).astype(jnp.int32)
    pl.semaphore_wait(pltpu.get_barrier_semaphore(), 4 + n_dp - self_target)

    pairs = [
        (source.at[:, head_lanes(1 - core, h)], buf.at[z, 0, h, own_rows], buf.at[z, 0, h, sib_rows])
        for source, buf, h in [(pk_in, kb, 0), (pk_in, kb, 1), (pv_in, vb, 0), (pv_in, vb, 1)]
    ] + [
        (q_in.at[:, sib_q], raw.at[0, 1], raw.at[0, 1]),
        (do_in.at[:, sib_q], raw.at[1, 1], raw.at[1, 1]),
        (o_in.at[:, sib_q], raw.at[2, 1], raw.at[2, 1]),
        (kc_in.at[:, sib_k], kvc.at[0, pl.ds(T, T)], kvc.at[0, pl.ds(T, T)]),
        (vc_in.at[:, sib_k], kvc.at[1, pl.ds(T, T)], kvc.at[1, pl.ds(T, T)]),
        (st_in, st.at[1], st.at[1]),
        (bias_own, bias.at[pl.ds(T, T)], bias.at[pl.ds(T, T)]),
    ]
    sends = [
        remote(src, dst, sib_s.at[i], sib_r.at[i], sib) for i, (src, dst, _) in enumerate(pairs)
    ]
    lands = [
        remote(land, land, sib_s.at[i], sib_r.at[i], sib) for i, (_, _, land) in enumerate(pairs)
    ]
    for i in range(4):
        sends[i].start()

    def hops(d, r):
        return half - r if d == 0 else half - 1 + r

    def place(d, s):
        return lax.rem(z + (n_z - s if d == 0 else s), n_z)

    def gather_send(buf, s_sem, r_sem, d, r, h, s):
        block = buf.at[place(d, s), r, h]
        return remote(block, block, s_sem.at[d, r, h, s + 1], r_sem.at[d, r, h, s + 1], ring[d])

    def gather_land(buf, s_sem, r_sem, d, r, h, s):
        block = buf.at[place(d, s), r, h]
        return remote(block, block, s_sem.at[d, r, h, s], r_sem.at[d, r, h, s], ring[d])

    def gather_start(buf, s_sem, r_sem, r, h):
        for d in (0, 1):
            gather_send(buf, s_sem, r_sem, d, r, h, 0).start()

    def across(src, dst, i):
        return remote(src, dst, y_s.at[i], y_r.at[i], ypart)

    def gather_step(buf, s_sem, r_sem, r, s, heads=range(HEADS)):
        for h in heads:
            for d in (0, 1):

                @pl.when((s >= 1) & (s <= hops(d, r)))
                def _():
                    gather_land(buf, s_sem, r_sem, d, r, h, s).wait_recv()

                @pl.when((s >= 1) & (s < hops(d, r)))
                def _():
                    gather_send(buf, s_sem, r_sem, d, r, h, s).start()

    def gather_drain(buf, s_sem, r_sem):
        for d in (0, 1):
            for r in (0, 1):

                def drain(s, carry):
                    for h in range(HEADS):
                        gather_send(buf, s_sem, r_sem, d, r, h, s).wait_send()
                    return carry

                lax.fori_loop(0, hops(d, r), drain, 0)

    def spots(s):
        return jnp.where((s == 0) | (s == half), 1, 2)

    def landed(*which):
        for i in which:
            copies[i].wait()
            lands[i].wait_recv()

    keys, values = (kb, k_s, k_r), (vb, v_s, v_r)
    crossings = [
        across(buf.at[z, 0, h], buf.at[z, 1, h], 2 * kind + h)
        for kind, buf in enumerate((kb, vb))
        for h in range(HEADS)
    ]
    for h in range(HEADS):
        landed(h)
        gather_start(*keys, 0, h)
        crossings[h].start()
    for i in (4, 7, 8, 10, 5, 6, 9):
        sends[i].start()
    for h in range(HEADS):
        landed(2 + h)
        crossings[2 + h].start()
        gather_start(*values, 0, h)

    def tiles(i, h, j):
        at = (h * GROUP + j) * HEAD_SIZE
        return jnp.concatenate([raw[i, 0, :, at : at + 128], raw[i, 1, :, at : at + 128]], 0)

    landed(4)
    for h in range(HEADS):
        for j in range(GROUP):
            rows = slice(j * BLOCK, (j + 1) * BLOCK)
            q_tile = tiles(0, h, j)
            qs[h, rows, :] = q_tile
            q_t[h, :, rows] = q_tile.T

    def merge(h, scores):
        old = top[h]
        new = jnp.maximum(old, jnp.max(scores, axis=0, keepdims=True))
        total[h] = total[h] * jnp.exp2(old - new) + jnp.sum(
            jnp.exp2(scores - new), axis=0, keepdims=True
        )
        top[h] = new

    landed(7, 8)
    lands[10].wait_recv()
    mask_tile = bias[...].astype(F32)
    for h in range(HEADS):
        scores = dot(kvc[0, :, h * 128 : (h + 1) * 128], q_t[h]) * (SCALE * LOG2E)
        scores = scores + jnp.concatenate([mask_tile] * GROUP, axis=1)
        sc[h] = scores
        new = jnp.max(scores, axis=0, keepdims=True)
        top[h] = new
        total[h] = jnp.sum(jnp.exp2(scores - new), axis=0, keepdims=True)
        dq_t[h] = jnp.zeros((HEAD_SIZE, ROWS), F32)

    def first_pass(s):
        def one(i, carry):
            pos = lax.rem(z + n_z + (1 - 2 * i) * s, n_z)
            for h in range(HEADS):
                block = kb[pos, :, h].reshape(2 * BLOCK, HEAD_SIZE)
                scores = dot(block, q_t[h]) * (SCALE * LOG2E)
                sbuf[h, pos] = scores
                merge(h, scores)
            return carry

        lax.fori_loop(0, spots(s), one, 0)

    landed(5, 6)
    for h in range(HEADS):
        for j in range(GROUP):
            rows = slice(j * BLOCK, (j + 1) * BLOCK)
            do_tile = tiles(1, h, j)
            dos[h, rows, :] = do_tile
            do_t[h, :, rows] = do_tile.T
            product = do_tile.astype(F32) * tiles(2, h, j).astype(F32)
            delta[h, :, rows] = jnp.sum(product.T, axis=0, keepdims=True)

    def gather_slot(i, carry):
        gather_step(*keys, 0, i)
        gather_step(*values, 0, i)
        for lag, chain in ((1, keys), (2, values)):

            @pl.when(i == lag)
            def _():
                for h in range(HEADS):
                    crossings[2 * lag - 2 + h].wait_recv()
                    gather_start(*chain, 1, h)

            gather_step(*chain, 1, i - lag)

        @pl.when(i <= half + 1)
        def _():
            first_pass(i - 1)

        return carry

    lax.fori_loop(1, half + 3, gather_slot, 0)
    for h in range(HEADS):
        top[h] = top[h] + jnp.log2(total[h])

    def key_terms(h, scores, key_block, value_block):
        probs = jnp.exp2(scores - top[h])
        dprobs = dot(value_block, do_t[h])
        dscores = (probs * (dprobs - delta[h])).astype(BF16)
        dv = dot(probs.astype(BF16), dos[h])
        dk = dot(dscores, qs[h]) * SCALE
        dq_t[h] += dot(key_block, dscores, 0, 0)
        return dk, dv

    def second_pass(s, h):
        def one(i, carry):
            pos = lax.rem(z + n_z + (1 - 2 * i) * s, n_z)
            key_block = kb[pos, :, h].reshape(2 * BLOCK, HEAD_SIZE)
            value_block = vb[pos, :, h].reshape(2 * BLOCK, HEAD_SIZE)
            dk, dv = key_terms(h, sbuf[h, pos], key_block, value_block)
            part[0, pos, :, h] = dk.reshape(2, BLOCK, HEAD_SIZE)
            part[1, pos, :, h] = dv.reshape(2, BLOCK, HEAD_SIZE)
            return carry

        lax.fori_loop(0, spots(s), one, 0)

    def sum_send(kind, d, r, h, s):
        return remote(
            sb.at[kind, d, r, h, s],
            rb.at[kind, d, r, h, s - 1],
            rs_s.at[kind, d, r, h, s],
            rs_r.at[kind, d, r, h, s - 1],
            ring[d],
        )

    def sum_land(kind, d, r, h, s):
        block = rb.at[kind, d, r, h, s]
        return remote(block, block, rs_s.at[kind, d, r, h, s], rs_r.at[kind, d, r, h, s], ring[d])

    def own_term(kind, d, r, h, s):
        return part[kind, place(1 - d, s), r, h]

    long_set = ((0, 0), (1, 1))
    short_set = ((1, 0), (0, 1))

    def sum_step(kind, pairs, s, first=False, heads=range(HEADS)):
        for h in heads:
            for d, r in pairs:
                term = own_term(kind, d, r, h, s)
                if not first:
                    sum_land(kind, d, r, h, s).wait_recv()
                    term = term + rb[kind, d, r, h, s].astype(F32)
                sb[kind, d, r, h, s] = term.astype(BF16)
                sum_send(kind, d, r, h, s).start()

    def arrived(kind, r, h):
        for d in (0, 1):
            sum_land(kind, d, r, h, 0).wait_recv()
        return (
            part[kind, z, r, h] + rb[kind, 0, r, h, 0].astype(F32) + rb[kind, 1, r, h, 0].astype(F32)
        )

    def sum_slot(u, carry):
        s = half - u
        for h in range(HEADS):
            second_pass(s, h)

            @pl.when(u == 0)
            def _():
                sum_step(0, long_set, s, True, (h,))

            @pl.when(u == 1)
            def _():
                sum_step(0, short_set, s, True, (h,))

            @pl.when((u > 1) & (s > 0))
            def _():
                sum_step(0, short_set, s, False, (h,))

        @pl.when((u > 0) & (s > 0))
        def _():
            sum_step(0, long_set, s)

        return carry

    lax.fori_loop(0, half + 1, sum_slot, 0)

    def swap(kind, r, h):
        yb[kind, r, h, 0] = arrived(kind, r, h).astype(BF16)
        i = 4 + (kind * 2 + r) * HEADS + h
        crossing = across(yb.at[kind, r, h, 0], yb.at[kind, 1 - r, h, 1], i)
        crossing.start()
        return crossing, across(yb.at[kind, r, h, 1], yb.at[kind, r, h, 1], 4 + (kind * 2 + 1 - r) * HEADS + h)

    swaps = {}
    for h in range(HEADS):
        swaps[0, 1, h] = swap(0, 1, h)
    sum_step(1, long_set, half, True)

    for h in range(HEADS):
        lanes = slice(h * 128, (h + 1) * 128)
        dk, dv = key_terms(h, sc[h], kvc[0, :, lanes], kvc[1, :, lanes])
        gkvc[0, :, lanes] = dk.astype(BF16)
        gkvc[1, :, lanes] = dv.astype(BF16)

    sum_step(1, short_set, half - 1, True)
    for h in range(HEADS):
        swaps[0, 0, h] = swap(0, 0, h)

    for h in range(HEADS):
        for j in range(GROUP):
            at = (h * GROUP + j) * HEAD_SIZE
            tile = (dq_t[h, :, j * BLOCK : (j + 1) * BLOCK].T * SCALE).astype(BF16)
            gqs[0, :, at : at + 128] = tile[:T]
            gqs[1, :, at : at + 128] = tile[T:]

    def give(i, src_own, src_sib, out, lanes):
        return (
            pltpu.make_async_copy(src_own, out.at[:, lanes], loc.at[i]),
            remote(src_sib, out.at[:, lanes], ret_s.at[i], ret_r.at[i], sib),
        )

    gives = [
        give(0, gqs.at[0], gqs.at[1], gq_out, own_q),
        give(1, gkvc.at[0, pl.ds(0, T)], gkvc.at[0, pl.ds(T, T)], gkc_out, own_k),
        give(2, gkvc.at[1, pl.ds(0, T)], gkvc.at[1, pl.ds(T, T)], gvc_out, own_k),
    ]
    for near, far in gives:
        near.start()
        far.start()

    sum_step(1, long_set, half - 1)
    copies[9].wait()
    lands[9].wait_recv()
    proj[...] = jnp.zeros(proj.shape, F32)
    grads = (dkb, dk_s, dk_r)

    def finish(kind, r, h):
        swaps[kind, r, h][1].wait_recv()
        near_sum = part[kind, z, r, h] + rb[kind, 0, r, h, 0].astype(F32)
        near_sum = near_sum + rb[kind, 1, r, h, 0].astype(F32)
        return (near_sum + yb[kind, r, h, 1].astype(F32)).astype(BF16)

    def give_prompt(i, buf, out, h):
        lanes = head_lanes(core, h)
        gives.append(give(i, buf.at[own_rows], buf.at[sib_rows], out, lanes))
        for copy in gives[-1]:
            copy.start()

    for r in (0, 1):
        for h in range(HEADS):
            dkb[z, r, h] = finish(0, r, h)
            gather_start(*grads, r, h)
            if r == 0:
                give_prompt(3 + h, dkb.at[z, 0, h], gpk_out, h)
        if r == 0:
            sum_step(1, short_set, half - 2)

    def project(h, s):
        def one(i, carry):
            pos = lax.rem(z + n_z + (1 - 2 * i) * s, n_z)
            for r in (0, 1):
                row = ((y if r == 0 else 1 - y) * n_z + pos) * BLOCK
                rows = pl.ds(pl.multiple_of(row, BLOCK), BLOCK)
                states = st[:, :, rows].reshape(2 * width, BLOCK)
                proj[h] += dot(states, dkb[pos, r, h])
            return carry

        lax.fori_loop(0, spots(s), one, 0)

    def proj_send(i_st, t):
        return remote(
            pack.at[i_st, t],
            prx.at[g],
            pj_s.at[i_st, t],
            pj_r.at[g],
            c if i_st == 0 else sib,
            core * per_core + t,
        )

    quarter = cols // 4
    lanes_at = lax.broadcasted_iota(jnp.int32, (quarter, HEAD_SIZE), 1) // 32
    per_head = per_core // HEADS

    def scatter(h):
        for i_st in (0, 1):
            turned = proj[h, i_st * width : (i_st + 1) * width].T
            head = turned[:, :128]
            tail = jnp.concatenate([turned[:, 128:], jnp.zeros((HEAD_SIZE, 96), F32)], axis=1)
            for k in range(per_head):
                t = h * per_head + k
                pack[i_st, t, :cols] = head[k * cols : (k + 1) * cols]
                folded = jnp.zeros((quarter, 128), F32)
                for j in range(4):
                    at = k * cols + j * quarter
                    piece = tail[at : at + quarter]
                    if j:
                        piece = pltpu.roll(piece, 32 * j, 1)
                    folded = jnp.where(lanes_at == j, piece, folded)
                pack[i_st, t, cols:] = folded

                @pl.when(core * per_core + t + i_st * n_dp != g)
                def _():
                    proj_send(i_st, t).start()

    def value_final():
        for h in range(HEADS):
            yb[1, 1, h, 0] = arrived(1, 1, h).astype(BF16)
            i = 4 + 3 * HEADS + h
            crossing = across(yb.at[1, 1, h, 0], yb.at[1, 0, h, 1], i)
            crossing.start()
            swaps[1, 0, h] = (crossing, across(yb.at[1, 0, h, 1], yb.at[1, 0, h, 1], i))

    rest = []
    for s in range(half - 2, 0, -1):
        rest.append((long_set, s))
        if s > 1:
            rest.append((short_set, s - 1))
    when = {0: (), 1: rest[:1], 2: rest[1:], 3: ()} if half > 3 else {half - 1: rest}

    for h in range(HEADS):
        project(h, 0)
    for s in range(1, half):
        gather_step(*grads, 0, s)
        gather_step(*grads, 1, s)
        for pairs, at in when.get(s, ()):
            sum_step(1, pairs, at)
        for h in range(HEADS):
            project(h, s)
        if s == half - 1:
            value_final()
    for h in range(HEADS):
        for r in (0, 1):
            gather_step(*grads, r, half, (h,))
        project(h, half)
        scatter(h)

    @pl.when(src_core == core)
    def _():
        prx[g] = pack[0, g - core * per_core]

    def collect(i, acc):
        @pl.when(jnp.logical_or(src_ctx != c, i != g))
        def _():
            remote(prx.at[i], prx.at[i], pj_s.at[0, 0], pj_r.at[i], sib).wait_recv()

        return acc + prx[i]

    summed = lax.fori_loop(0, n_dp, collect, jnp.zeros(prx.shape[1:], F32))
    gproj_out[:, :128] = summed[:cols]
    for j in range(4):
        piece = summed[cols:]
        if j:
            piece = pltpu.roll(piece, 128 - 32 * j, 1)
        gproj_out[j * quarter : (j + 1) * quarter, 128:] = piece[:, :32]

    for h in range(HEADS):
        arrived(1, 0, h)
        dvf[h] = finish(1, 0, h)
        give_prompt(3 + HEADS + h, dvf.at[h], gpv_out, h)

    def scatter_drain(t, carry):
        @pl.when(core * per_core + t != g)
        def _():
            proj_send(0, t).wait_send()

        proj_send(1, t).wait_send()
        return carry

    lax.fori_loop(0, per_core, scatter_drain, 0)
    for send in sends:
        send.wait_send()
    for chain in (keys, values, grads):
        gather_drain(*chain)
    for crossing in crossings:
        crossing.wait_send()
    for crossing, _ in swaps.values():
        crossing.wait_send()
    for kind in (0, 1):
        for d in (0, 1):
            for r in (0, 1):

                def drain(s, carry):
                    for h in range(HEADS):
                        sum_send(kind, d, r, h, s).wait_send()
                    return carry

                lax.fori_loop(1, hops(d, r) + 1, drain, 0)
    for near, far in gives:
        near.wait()
        far.wait()


def hand_on(*refs):
    count = len(refs) // 2
    for source, target in zip(refs[:count], refs[count:]):
        target[...] = source[...]


def body(q, do, o, kc, vc, pk, pv, states, lengths):
    n_ctx = lax.axis_size("ctx")
    n_dp = lax.axis_size("dp")
    n_z = n_ctx // 4
    half = n_z // 2
    prompt = states.shape[1]
    width = states.shape[2]
    cols = KEY_HEAD_COUNT * HEAD_SIZE // n_dp
    hbm = pl.BlockSpec(memory_space=pl.ANY)
    dma = pltpu.SemaphoreType.DMA
    out = pl.pallas_call(
        functools.partial(kernel, n_z, n_dp),
        out_shape=[
            jax.ShapeDtypeStruct(q.shape[1:], BF16),
            jax.ShapeDtypeStruct(kc.shape[1:], BF16),
            jax.ShapeDtypeStruct(vc.shape[1:], BF16),
            jax.ShapeDtypeStruct(pk.shape[1:], BF16),
            jax.ShapeDtypeStruct(pv.shape[1:], BF16),
            jax.ShapeDtypeStruct((cols, width), F32),
        ],
        in_specs=[hbm] * 8 + [pl.BlockSpec(memory_space=pltpu.SMEM)],
        out_specs=[hbm] * 5 + [pl.BlockSpec(memory_space=pltpu.VMEM)],
        scratch_shapes=[
            pltpu.VMEM((n_z, 2, HEADS, BLOCK, HEAD_SIZE), BF16),
            pltpu.VMEM((n_z, 2, HEADS, BLOCK, HEAD_SIZE), BF16),
            pltpu.VMEM((3, 2, T, QW), BF16),
            pltpu.VMEM((2, BLOCK, KW), BF16),
            pltpu.VMEM((T, BLOCK), BF16),
            pltpu.VMEM((BLOCK, BLOCK), BF16),
            pltpu.VMEM((2, width, prompt), BF16),
            pltpu.VMEM((HEADS, ROWS, HEAD_SIZE), BF16),
            pltpu.VMEM((HEADS, ROWS, HEAD_SIZE), BF16),
            pltpu.VMEM((HEADS, HEAD_SIZE, ROWS), BF16),
            pltpu.VMEM((HEADS, HEAD_SIZE, ROWS), BF16),
            pltpu.VMEM((HEADS, 1, ROWS), F32),
            pltpu.VMEM((HEADS, 1, ROWS), F32),
            pltpu.VMEM((HEADS, 1, ROWS), F32),
            pltpu.VMEM((HEADS, n_z, 2 * BLOCK, ROWS), F32),
            pltpu.VMEM((HEADS, BLOCK, ROWS), F32),
            pltpu.VMEM((HEADS, HEAD_SIZE, ROWS), F32),
            pltpu.VMEM((2, n_z, 2, HEADS, BLOCK, HEAD_SIZE), F32),
            pltpu.VMEM((2, 2, 2, HEADS, half + 1, BLOCK, HEAD_SIZE), BF16),
            pltpu.VMEM((2, 2, 2, HEADS, half + 1, BLOCK, HEAD_SIZE), BF16),
            pltpu.VMEM((2, 2, HEADS, 2, BLOCK, HEAD_SIZE), BF16),
            pltpu.VMEM((n_z, 2, HEADS, BLOCK, HEAD_SIZE), BF16),
            pltpu.VMEM((HEADS, BLOCK, HEAD_SIZE), BF16),
            pltpu.VMEM((HEADS, 2 * width, HEAD_SIZE), F32),
            pltpu.VMEM((2, n_dp // 2, cols + cols // 4, 128), F32),
            pltpu.VMEM((n_dp, cols + cols // 4, 128), F32),
            pltpu.VMEM((2, T, QW), BF16),
            pltpu.VMEM((2, BLOCK, KW), BF16),
            dma((10,)),
            dma((11,)),
            dma((11,)),
            dma((12,)),
            dma((12,)),
            *[dma((2, 2, HEADS, half + 1))] * 4,
            dma((2, 2, 2, HEADS, half + 1)),
            dma((2, 2, 2, HEADS, half + 1)),
            *[dma((2, 2, HEADS, half + 1))] * 2,
            dma((2, n_dp // 2)),
            dma((n_dp,)),
            dma((7,)),
            dma((7,)),
        ],
        compiler_params=pltpu.CompilerParams(
            collective_id=0, has_side_effects=True, vmem_limit_bytes=56 * 2**20
        ),
    )(q[0], do[0], o[0], kc[0], vc[0], pk[0], pv[0], states[0].T, lengths[0, 0])
    out = pl.pallas_call(
        hand_on,
        out_shape=[jax.ShapeDtypeStruct(x.shape, x.dtype) for x in out],
    )(*out)
    return (*(x[None] for x in out[:5]), out[5].T)


def solution(mesh):
    split = P("dp", "ctx", None)
    return jax.shard_map(
        body,
        mesh=mesh,
        in_specs=(split,) * 7 + (P("dp", None, "ctx"), split),
        out_specs=(split,) * 5 + (P("ctx", "dp"),),
        check_vma=False,
    )
```
